512 devices in a mesh: expert: 32 (over x, z), seq: 8 (over y), dp: 2 (over core).
Axes of the slice: x: 4, y: 8, z: 8, core: 2. Of those that a mesh axis runs over, the one named last changes fastest.
Arguments:
- moe_input: bfloat16 [65536, 2048], P(('expert', 'seq', 'dp')), may hold values from -6 to 6
- lm_grad: bfloat16 [65536, 2048], P(('expert', 'seq', 'dp')), may hold values from -6 to 6
- frame_grad: bfloat16 [16384, 2048], P(('expert', 'seq', 'dp')), may hold values from -6 to 6
- span_token: int32 [4096], P(('expert', 'seq', 'dp')), may hold values from 0 to 1023
- expert_ids: int32 [65536, 2], P(('expert', 'seq', 'dp')), may hold values from 0 to 31, all different within a row; in each aligned block of 128 rows (0 to 127, 128 to 255, ...) at most 16 rows name the same one
- gate_weights: bfloat16 [65536, 2], P(('expert', 'seq', 'dp')), may hold values from 0.049804688 to 0.5
- w_gate_up: bfloat16 [32, 2048, 2, 384], P('expert', ('seq', 'dp')), may hold values from -0.125 to 0.125
- w_down: bfloat16 [32, 2048, 384], P('expert', ('seq', 'dp')), may hold values from -0.3125 to 0.3125
Outputs:
- grad_input: bfloat16 [65536, 2048], P(('expert', 'seq', 'dp'))
- grad_gates: bfloat16 [65536, 2], P(('expert', 'seq', 'dp'))
- grad_gate_up: float32 [32, 2048, 2, 384], P('expert', ('seq', 'dp'))
The draws below stay inside these ranges and needn't reach their ends.
Inputs may be any that keep to these rules, and one draw needn't show every extreme that they name: `span_token`: every value names a token of the span's own dialogue group. `expert_ids`: A token's experts are distinct. Of one device's rows at most 16 name one expert, and in every draw some expert is named by exactly 16 rows of some device.
All inputs are finite; a program needn't handle non-finite values.
Results may differ from the reference program's by a relative error of at most 0.02.
Values may be sent and summed in bfloat16 or wider, within the bound.
No kernel may reach another device: no remote copies, remote signals or barrier semaphores. Data moves between devices by JAX's collectives and lax.ppermute only.
A program may use at most 64 MiB of HBM per device.

```python
import math
import jax
import jax.numpy as jnp
import numpy as np
from jax import lax

D = 2048
FF = 384
TOPW = 2
TOK_DEV = 128
CHK_DEV = 8
CHF = 4
FR_DEV = 32
EXPERTS = 32
CAP = 16
TOKENS = 65536
FRAMES = 16384
SPANS = 4096
N_EXPERT = 32
N_SEQ = 8
N_DP = 2


def plant(entries, rng, smallest, high):
    index_at = [jax.random.randint(jax.random.fold_in(rng, axis), (), 0, length) for axis, length in enumerate(entries.shape)]
    widest = entries.shape.index(max(entries.shape))
    next_to = index_at[:widest] + [(index_at[widest] + 1) % entries.shape[widest]] + index_at[widest + 1:]
    return entries.at[tuple(index_at)].set(smallest).at[tuple(next_to)].set(high)


def shard_levels(key, extent, cuts, smallest, largest):
    gain, own = 1.0, jax.random.fold_in(key, 6)
    for dim, blocks in cuts:
        steps = jnp.exp(jax.random.uniform(jax.random.fold_in(own, dim), (blocks,), jnp.float32, smallest / len(cuts), largest / len(cuts)))
        gain = gain * jnp.repeat(steps, extent[dim] // blocks).reshape([-1 if axis == dim else 1 for axis in range(len(extent))])
    return gain


def rank_table(number_of, lean):
    loads = [(1 << 20) // math.isqrt(grade ** lean) + 1 for grade in range(1, number_of + 1)]
    spread = 1 + sum(loads) // (1 << 30)
    return np.cumsum(np.array([max(1, weight // spread) for weight in loads]))


def ranked_ids(stream_key, extent, amount, skew):
    grid = rank_table(amount, skew)
    pick = jax.random.randint(jax.random.fold_in(stream_key, 1), extent, 0, int(grid[amount - 1]))
    rank = jnp.searchsorted(jnp.asarray(grid, jnp.int32), pick, side="right")
    return jax.random.permutation(jax.random.fold_in(stream_key, 2), amount)[rank].astype(jnp.int32)


def deal_out(rng, own, number, rows, count, top, limit, skew):
    sequence = jax.random.permutation(rng, count)
    packed, usual = shares(count, rows * top, limit, skew, True), shares(count, rows * top, limit, skew, False)
    places = jnp.arange(count)

    def named(sizes, rotation):
        used = int((sizes > 0).sum())
        fixed = max(1, used // 4)
        shifted = fixed + (places - fixed + rotation * (used - fixed)) % max(1, count - fixed)
        return jnp.zeros((count,), jnp.int32).at[sequence[jnp.where(places < fixed, places, shifted)]].set(jnp.asarray(sizes, jnp.int32))

    sizes = jnp.where(number % 4 == 0, named(packed, number // 4), named(usual, number - number // 4 - 1))
    mixed = jax.random.permutation(jax.random.fold_in(own, 3), count)
    source_of, taker = mixed[0:count // 2 * 2:2], mixed[1:count // 2 * 2:2]
    margin = jnp.minimum(sizes[source_of] - 1, limit - sizes[taker]) // 2
    margin = jnp.where((source_of == sequence[0]) | (taker == sequence[0]) | (sizes[taker] == 0), 0, jnp.maximum(margin, 0))
    shifted = jax.random.randint(jax.random.fold_in(own, 4), (count // 2,), 0, 1 << 20) % (margin + 1)
    sizes = sizes.at[source_of].add(-shifted).at[taker].add(shifted)
    members = jnp.searchsorted(jnp.cumsum(sizes), jnp.arange(rows * top), side="right").astype(jnp.int32)
    grid = members.reshape(top, rows).T
    grid = grid[jax.random.permutation(jax.random.fold_in(own, 1), rows)]
    rotation = jax.random.randint(jax.random.fold_in(own, 2), (rows, 1), 0, top)
    return jnp.take_along_axis(grid, (jnp.arange(top)[None, :] + rotation) % top, axis=1)


def shares(count, total, reach, skew, full):
    portions = [(1 << 20) // math.isqrt(standing ** skew) + 1 for standing in range(1, count + 1)]
    largest = reach if full else min(reach, max(-(-total // count), total * portions[0] // sum(portions)))
    least = 1 if total - largest >= count - 1 else 0
    counts, spare = [largest] + [least] * (count - 1), total - largest - least * (count - 1)
    while spare > 0:
        free = [i for i in range(1, count) if counts[i] < largest] or [i for i in range(1, count) if counts[i] < reach]
        pool, left = sum([portions[i] for i in free]), spare
        for i in free:
            more = min(reach - counts[i], max(1, left * portions[i] // pool), spare)
            counts[i] = counts[i] + more
            spare = spare - more
    return np.array(counts)


def noise(rng, extent, scale, bound, cuts=(), kind=jnp.bfloat16):
    values = jax.random.normal(rng, extent, jnp.float32) * scale
    if len(cuts) > 0:
        values = shard_levels(rng, extent, cuts, -0.22, 0.18) * values
    return jnp.clip(values, min=-bound, max=bound).astype(kind)


def setup_inputs(seed: int = 0) -> dict:
    keys = jax.random.split(jax.random.key(seed), 9)
    moe_input = noise(keys[0], (TOKENS, D), 1.0, 6.0, ((0, 512),))
    lm_grad = noise(keys[1], (TOKENS, D), 1.0, 6.0, ((0, 512),))
    frame_grad = noise(keys[2], (FRAMES, D), 1.0, 6.0, ((0, 512),))
    span_token = plant(ranked_ids(keys[3], (SPANS,), TOK_DEV * N_SEQ, 2), jax.random.fold_in(keys[3], 3), 0, (TOK_DEV * N_SEQ) - 1).astype(jnp.int32)
    expert_ids_keys = jax.random.split(jax.random.fold_in(keys[4], 1), TOKENS // TOK_DEV)
    expert_ids_turns = jax.random.permutation(jax.random.fold_in(keys[4], 3), TOKENS // TOK_DEV)
    expert_ids = jax.vmap(lambda own, number: deal_out(jax.random.fold_in(keys[4], 2), own, number, TOK_DEV, EXPERTS, TOPW, CAP, 2))(expert_ids_keys, expert_ids_turns).reshape((TOKENS, TOPW))
    gate_weights = jnp.clip(0.049804688 + 0.4501953 * jax.random.uniform(keys[5], (TOKENS, TOPW), jnp.float32) ** shard_levels(keys[5], (TOKENS, TOPW), ((0, 512),), -0.2, 0.2), 0.049804688, 0.5).astype(jnp.bfloat16)
    w_gate_up = noise(keys[6], (EXPERTS, D, 2, FF), D ** -0.5, 0.125, ((0, 32), (1, 16)))
    w_down = noise(keys[7], (EXPERTS, D, FF), FF ** -0.5, 0.3125, ((0, 32), (1, 16)))
    return dict(moe_input=moe_input, lm_grad=lm_grad, frame_grad=frame_grad, span_token=span_token, expert_ids=expert_ids, gate_weights=gate_weights, w_gate_up=w_gate_up, w_down=w_down)


def to_groups(values):
    shaped = values.reshape((N_EXPERT, N_SEQ, N_DP, TOK_DEV) + values.shape[1:])
    moved = jnp.moveaxis(shaped, 0, 2)
    return moved.reshape((N_SEQ * N_DP, N_EXPERT, TOK_DEV) + values.shape[1:])


def from_groups(values):
    shaped = values.reshape((N_SEQ, N_DP, N_EXPERT, TOK_DEV) + values.shape[3:])
    moved = jnp.moveaxis(shaped, 2, 0)
    return moved.reshape((TOKENS,) + values.shape[3:])


def slot_targets(slot_expert):
    member = (slot_expert[..., None] == jnp.arange(N_EXPERT, dtype=jnp.int32)).astype(jnp.int32)
    position = jnp.sum((jnp.cumsum(member, axis=-2) - member) * member, axis=-1).astype(jnp.int32)
    return (slot_expert * CAP + position).astype(jnp.int32)


def place_rows(values, target):
    shape = (N_EXPERT * CAP,) + values.shape[1:]
    return jnp.zeros(shape, values.dtype).at[target].set(values)


def to_expert(values):
    rest = values.shape[2:]
    shaped = values.reshape((N_EXPERT, N_EXPERT, CAP) + rest)
    return jnp.swapaxes(shaped, 0, 1).reshape((N_EXPERT, N_EXPERT * CAP) + rest)


def take_rows(values, target):
    return values[target]


def reference(moe_input, lm_grad, frame_grad, span_token, expert_ids, gate_weights, w_gate_up, w_down):
    group_tokens = TOK_DEV * N_SEQ
    frames = jnp.moveaxis(frame_grad.reshape(N_EXPERT, N_SEQ, N_DP, FR_DEV, D), 1, 2)
    frames = frames.reshape(N_EXPERT * N_DP, N_SEQ * FR_DEV, D)
    spans = jnp.moveaxis(span_token.reshape(N_EXPERT, N_SEQ, N_DP, CHK_DEV), 1, 2)
    spans = spans.reshape(N_EXPERT * N_DP, N_SEQ * CHK_DEV)
    frame_ids = jnp.repeat(spans, CHF, axis=1).astype(jnp.int32)

    def one_group(pair):
        rows, names = pair
        return jax.ops.segment_sum(rows.astype(jnp.float32), names, num_segments=group_tokens)

    cond_sum = lax.map(one_group, (frames, frame_ids))
    cond_sum = jnp.moveaxis(cond_sum.reshape(N_EXPERT, N_DP, N_SEQ, TOK_DEV, D), 1, 2).reshape(TOKENS, D)
    upstream = (lm_grad.astype(jnp.float32) + cond_sum).astype(jnp.bfloat16)

    gate_up32 = w_gate_up.astype(jnp.float32)
    down32 = w_down.astype(jnp.float32)
    slot_token = jnp.arange(TOK_DEV * TOPW, dtype=jnp.int32) // TOPW

    def expert_group(carry, inputs):
        group_input, group_grad, group_ids, group_gate = inputs
        target = slot_targets(group_ids.reshape(N_EXPERT, TOK_DEV * TOPW))
        send_input = jax.vmap(place_rows)(group_input[:, slot_token], target)
        send_grad = jax.vmap(place_rows)(group_grad[:, slot_token], target)
        send_gate = jax.vmap(place_rows)(group_gate.reshape(N_EXPERT, TOK_DEV * TOPW), target)
        slot_input = to_expert(send_input)
        slot_grad = to_expert(send_grad)
        slot_gate = to_expert(send_gate).astype(jnp.float32)
        pre_acts = jnp.einsum("erd,edcf->ercf", slot_input.astype(jnp.float32), gate_up32)
        gate_pre = pre_acts[:, :, 0]
        up_pre = pre_acts[:, :, 1]
        sigmoid_gate = jax.nn.sigmoid(gate_pre)
        activated = gate_pre * sigmoid_gate
        hidden = (activated * up_pre).astype(jnp.bfloat16)
        expert_out = jnp.einsum("erf,edf->erd", hidden.astype(jnp.float32), down32)
        grad_float = slot_grad.astype(jnp.float32)
        gate_grad_slot = jnp.sum(grad_float * expert_out, axis=-1).astype(jnp.bfloat16)
        scaled_grad = (slot_gate[..., None] * grad_float).astype(jnp.bfloat16)
        hidden_grad = jnp.einsum("erd,edf->erf", scaled_grad.astype(jnp.float32), down32)
        slope = sigmoid_gate * (1.0 + gate_pre * (1.0 - sigmoid_gate))
        pre_grad = jnp.stack([hidden_grad * up_pre * slope, hidden_grad * activated], axis=2).astype(jnp.bfloat16)
        input_grad = jnp.einsum("ercf,edcf->erd", pre_grad.astype(jnp.float32), gate_up32).astype(jnp.bfloat16)
        partial_value = jnp.einsum("erd,ercf->edcf", slot_input.astype(jnp.float32), pre_grad.astype(jnp.float32))
        partial_value = lax.optimization_barrier(partial_value.astype(jnp.bfloat16)).astype(jnp.float32)
        back_input = to_expert(input_grad)
        back_gate = to_expert(gate_grad_slot)
        slot_back = jax.vmap(take_rows)(back_input, target)
        gate_back = jax.vmap(take_rows)(back_gate, target)
        summed = jnp.sum(slot_back.reshape(N_EXPERT, TOK_DEV, TOPW, D).astype(jnp.float32), axis=2)
        return carry + partial_value, (summed.astype(jnp.bfloat16), gate_back.reshape(N_EXPERT, TOK_DEV, TOPW))

    start = jnp.zeros((N_EXPERT, D, 2, FF), jnp.float32)
    inputs = (to_groups(moe_input), to_groups(upstream), to_groups(expert_ids), to_groups(gate_weights))
    grad_gate_up, (grouped_input, grouped_gates) = lax.scan(expert_group, start, inputs)
    return from_groups(grouped_input), from_groups(grouped_gates), grad_gate_up
```

```python
import functools

import jax
import jax.numpy as jnp
from jax import lax
from jax.experimental import pallas as pl
from jax.experimental.pallas import tpu as pltpu
from jax.sharding import PartitionSpec as P

F32 = jnp.float32
BF16 = jnp.bfloat16
NT = (((1,), (1,)), ((), ()))
NN = (((1,), (0,)), ((), ()))


def mm(a, b, dims=NN):
    return lax.dot_general(a, b, dims, preferred_element_type=F32)


def one_hot(target, rows):
    tokens = target.shape[1]
    return lax.broadcasted_iota(jnp.int32, (rows, tokens), 0) == target


def route_kernel(experts, cap, ids_ref, gate_ref, x_ref, send_ref, target_ref, gate_out_ref):
    tokens = ids_ref.shape[1]
    ids = ids_ref[...]
    members = [
        (lax.broadcasted_iota(jnp.int32, (experts, tokens), 0) == ids[k : k + 1]).astype(F32)
        for k in range(2)
    ]
    earlier = (
        lax.broadcasted_iota(jnp.int32, (tokens, tokens), 0)
        < lax.broadcasted_iota(jnp.int32, (tokens, tokens), 1)
    ).astype(BF16)
    count = mm((members[0] + members[1]).astype(BF16), earlier)
    rows = experts * cap
    gates = jnp.zeros((1, rows), F32)
    select = None
    for k in range(2):
        position = jnp.sum(members[k] * count, axis=0, keepdims=True).astype(jnp.int32)
        target = ids[k : k + 1] * cap + position
        target_ref[k : k + 1, :] = target
        hot = one_hot(target, rows)
        hot_k = hot.astype(F32)
        gate = jnp.broadcast_to(gate_ref[k : k + 1, :].astype(F32), (8, tokens)).astype(BF16)
        gates += mm(gate, hot_k.astype(BF16), NT)[0:1]
        select = hot_k if select is None else select + hot_k
    gate_out_ref[...] = gates.astype(BF16)
    send_ref[...] = mm(select.astype(BF16), x_ref[...]).astype(BF16)


def upstream_kernel(span, own_ref, names_ref, frames_ref, lm_ref, target_ref, send_ref):
    tokens = lm_ref.shape[0]
    frames = frames_ref.shape[0]
    first = own_ref[0]
    own = lax.broadcasted_iota(jnp.int32, (tokens, frames), 0) + first
    named = (own == names_ref[...]).astype(F32).astype(BF16)
    upstream = (lm_ref[...].astype(F32) + mm(named, frames_ref[...])).astype(BF16)
    rows = send_ref.shape[0]
    select = one_hot(target_ref[0:1, :], rows).astype(F32)
    select += one_hot(target_ref[1:2, :], rows).astype(F32)
    send_ref[...] = mm(select.astype(BF16), upstream).astype(BF16)


def forward_kernel(ff, x_ref, w_ref, hidden_ref, gate_term_ref, up_term_ref):
    pre = mm(x_ref[...], w_ref[:, : 2 * ff])
    gate_pre = pre[:, :ff]
    up_pre = pre[:, ff:]
    sig = jax.nn.sigmoid(gate_pre)
    activated = gate_pre * sig
    slope = sig * (1.0 + gate_pre * (1.0 - sig))
    hidden_ref[...] = (activated * up_pre).astype(BF16)
    gate_term_ref[...] = up_pre * slope
    up_term_ref[...] = activated


def backward_kernel(
    ff, y_ref, wd_ref, w_ref, gate_ref, hidden_ref, gate_term_ref, up_term_ref,
    out_ref, pre_ref, gate_grad_ref,
):
    @pl.when(pl.program_id(0) == 0)
    def _():
        down = mm(y_ref[...], wd_ref[...])
        gate_grad_ref[...] = jnp.sum(
            hidden_ref[...].astype(F32) * down, axis=1, keepdims=True
        )
        hidden_grad = down * gate_ref[...]
        pre_ref[:, :ff] = (hidden_grad * gate_term_ref[...]).astype(BF16)
        pre_ref[:, ff:] = (hidden_grad * up_term_ref[...]).astype(BF16)

    out_ref[...] = mm(pre_ref[...], w_ref[...], NT).astype(BF16)


def combine_kernel(back_ref, target_ref, column_ref, gate_ref, out_ref, gate_out_ref):
    rows = back_ref.shape[0]
    tokens = out_ref.shape[0]
    place = lax.broadcasted_iota(jnp.int32, (tokens, rows), 1)
    pick = (place == column_ref[:, 0:1]).astype(F32) + (place == column_ref[:, 1:2]).astype(F32)
    out_ref[...] = mm(pick.astype(BF16), back_ref[...]).astype(BF16)
    gates = jnp.broadcast_to(gate_ref[...].astype(F32), (8, rows)).astype(BF16)
    for k in range(2):
        hot = one_hot(target_ref[k : k + 1, :], rows).astype(F32).astype(BF16)
        gate_out_ref[k : k + 1, :] = mm(gates, hot)[0:1].astype(BF16)


def whole(shape, space=pltpu.VMEM):
    return pl.BlockSpec(shape, lambda *_: (0,) * len(shape), memory_space=space)


def call(kernel, outs, args, limit=24, **kw):
    return pl.pallas_call(
        kernel,
        out_shape=outs,
        compiler_params=pltpu.CompilerParams(vmem_limit_bytes=limit << 20),
        **kw,
    )(*args)


def on_device(moe_input, lm_grad, frame_grad, span_token, expert_ids, gate_weights, w_gate_up, w_down):
    tokens, width = moe_input.shape
    per_span = frame_grad.shape[0] // span_token.shape[0]
    experts = lax.axis_size("expert")
    n_seq = lax.axis_size("seq")
    cap = 2 * tokens * expert_ids.shape[1] // experts
    rows = experts * cap
    ff = w_down.shape[2]
    me = lax.axis_index("expert")
    sds = jax.ShapeDtypeStruct

    def exchange(values):
        return lax.all_to_all(
            values.reshape(experts, cap, width), "expert", split_axis=0, concat_axis=0, tiled=True
        ).reshape(rows, width)

    frame_rows = lax.all_gather(frame_grad, "seq", axis=0, tiled=True)

    send_input, target, send_gate = call(
        functools.partial(route_kernel, experts, cap),
        (sds((rows, width), BF16), sds((2, tokens), jnp.int32), sds((1, rows), BF16)),
        (expert_ids.T, gate_weights.T, moe_input),
    )
    got_input = exchange(send_input)

    span_names = lax.all_gather(span_token, "seq", axis=0, tiled=True)
    all_gates = lax.all_gather(send_gate, "expert", axis=0, tiled=True)
    slot_gate = lax.dynamic_slice(all_gates, (0, me * cap), (experts, cap))
    slot_gate = slot_gate.astype(F32).reshape(rows, 1)

    weights = jnp.concatenate([w_gate_up.reshape(-1, 2 * ff), w_down[0]], axis=1)
    weights = lax.all_gather(weights, ("seq", "dp"), axis=0, tiled=True)

    frame_names = jnp.repeat(span_names, per_span)[None, :]
    own = (lax.axis_index("seq") * tokens).reshape(1)
    send_grad = call(
        functools.partial(upstream_kernel, per_span),
        sds((rows, width), BF16),
        (own, frame_names, frame_rows, lm_grad, target),
        in_specs=[pl.BlockSpec(memory_space=pltpu.SMEM)]
        + [pl.BlockSpec(memory_space=pltpu.VMEM)] * 4,
    )
    got_grad = exchange(send_grad)

    hidden, gate_term, up_term = call(
        functools.partial(forward_kernel, ff),
        (sds((rows, ff), BF16), sds((rows, ff), F32), sds((rows, ff), F32)),
        (got_input, weights),
    )
    block = width // 4
    input_grad, pre_grad, gate_grad = call(
        functools.partial(backward_kernel, ff),
        (sds((rows, width), BF16), sds((rows, 2 * ff), BF16), sds((rows, 1), F32)),
        (got_grad, weights, weights, slot_gate, hidden, gate_term, up_term),
        grid=(4,),
        in_specs=[
            whole((rows, width)),
            pl.BlockSpec((width, ff), lambda j: (0, 2)),
            pl.BlockSpec((block, 2 * ff), lambda j: (j, 0)),
            whole((rows, 1)),
            whole((rows, ff)),
            whole((rows, ff)),
            whole((rows, ff)),
        ],
        out_specs=[
            pl.BlockSpec((rows, block), lambda j: (0, j)),
            whole((rows, 2 * ff)),
            whole((rows, 1)),
        ],
    )
    back_input = exchange(input_grad)
    all_gate_grad = lax.all_gather(gate_grad.astype(BF16).reshape(1, rows), "expert", axis=0, tiled=True)
    back_gate = lax.dynamic_slice(all_gate_grad, (0, me * cap), (experts, cap)).reshape(1, rows)

    partial = lax.dot_general(
        got_input, pre_grad, (((0,), (0,)), ((), ())), preferred_element_type=F32
    ).astype(BF16)
    partial = partial.reshape(n_seq, 2, -1, 2 * ff)
    core = lax.axis_index("dp")
    mine = lax.dynamic_index_in_dim(partial, core, 1, keepdims=False)
    other = lax.dynamic_index_in_dim(partial, 1 - core, 1, keepdims=False)
    other = lax.ppermute(other, "dp", [(0, 1), (1, 0)])
    pair = (mine.astype(F32) + other.astype(F32)).astype(BF16)
    grad = lax.psum_scatter(pair, "seq", scatter_dimension=0, tiled=True).astype(F32)
    grad_gate_up = grad.reshape(1, -1, 2, ff)

    grad_input, grad_gates = call(
        combine_kernel,
        (sds((tokens, width), BF16), sds((2, tokens), BF16)),
        (back_input, target, target.T, back_gate),
    )
    return grad_input, grad_gates.T, grad_gate_up


def solution(mesh):
    every = ("expert", "seq", "dp")
    return jax.shard_map(
        on_device,
        mesh=mesh,
        in_specs=(
            P(every, None),
            P(every, None),
            P(every, None),
            P(every),
            P(every, None),
            P(every, None),
            P("expert", ("seq", "dp"), None, None),
            P("expert", ("seq", "dp"), None),
        ),
        out_specs=(P(every, None), P(every, None), P("expert", ("seq", "dp"), None, None)),
        check_vma=False,
    )
```

```python
import functools

import jax
import jax.numpy as jnp
from jax import lax
from jax.experimental import pallas as pl
from jax.experimental.pallas import tpu as pltpu
from jax.sharding import PartitionSpec as P

F32 = jnp.float32
BF16 = jnp.bfloat16
NT = (((1,), (1,)), ((), ()))
NN = (((1,), (0,)), ((), ()))


def mm(a, b, dims=NN):
    return lax.dot_general(a, b, dims, preferred_element_type=F32)


def one_hot(target, rows):
    tokens = target.shape[1]
    return lax.broadcasted_iota(jnp.int32, (rows, tokens), 0) == target


def route_kernel(experts, cap, ids_ref, x_ref, send_ref, target_ref):
    tokens = ids_ref.shape[1]
    ids = ids_ref[...]
    members = [
        (lax.broadcasted_iota(jnp.int32, (experts, tokens), 0) == ids[k : k + 1]).astype(F32)
        for k in range(2)
    ]
    earlier = (
        lax.broadcasted_iota(jnp.int32, (tokens, tokens), 0)
        < lax.broadcasted_iota(jnp.int32, (tokens, tokens), 1)
    ).astype(F32)
    count = mm((members[0] + members[1]).astype(BF16), earlier.astype(BF16))
    rows = experts * cap
    select = None
    for k in range(2):
        position = jnp.sum(members[k] * count, axis=0, keepdims=True).astype(jnp.int32)
        target = ids[k : k + 1] * cap + position
        target_ref[k : k + 1, :] = target
        hot = one_hot(target, rows).astype(F32)
        select = hot if select is None else select + hot
    send_ref[...] = mm(select.astype(BF16), x_ref[...]).astype(BF16)


def upstream_kernel(own_ref, frames_ref, lm_ref, target_ref, gate_ref, send_ref):
    tokens, width = lm_ref.shape
    frames = frames_ref.shape[0]
    coded = frames_ref[:, width:].astype(F32)
    name = (coded[:, 0:1] * 32.0 + coded[:, 1:2]).astype(jnp.int32) - own_ref[0]
    named = (lax.broadcasted_iota(jnp.int32, (frames, tokens), 1) == name).astype(F32)
    cond = mm(named.T.astype(BF16), frames_ref[:, :width])
    upstream = (lm_ref[...].astype(F32) + cond).astype(BF16)
    rows = send_ref.shape[0]
    hot = [one_hot(target_ref[k : k + 1, :], rows).astype(F32) for k in range(2)]
    gates = gate_ref[...].astype(F32)
    gate = jnp.sum(hot[0] * gates[0:1] + hot[1] * gates[1:2], axis=1, keepdims=True)
    send_ref[...] = (mm((hot[0] + hot[1]).astype(BF16), upstream) * gate).astype(BF16)


def forward_kernel(ff, x_ref, w_ref, hidden_ref, gate_term_ref, up_term_ref):
    pre = mm(x_ref[...], w_ref[:, : 2 * ff])
    gate_pre = pre[:, :ff]
    up_pre = pre[:, ff:]
    sig = jax.nn.sigmoid(gate_pre)
    activated = gate_pre * sig
    slope = sig * (1.0 + gate_pre * (1.0 - sig))
    hidden_ref[...] = (activated * up_pre).astype(BF16)
    gate_term_ref[...] = up_pre * slope
    up_term_ref[...] = activated


def backward_kernel(ff, y_ref, w_ref, hidden_ref, gate_term_ref, up_term_ref, out_ref, pre_ref):
    rows, width = y_ref.shape
    hidden_grad = mm(y_ref[...], w_ref[:, 2 * ff :])
    pre_ref[:, :ff] = (hidden_grad * gate_term_ref[...]).astype(BF16)
    pre_ref[:, ff:] = (hidden_grad * up_term_ref[...]).astype(BF16)
    total = jnp.sum(hidden_ref[...].astype(F32) * hidden_grad, axis=1, keepdims=True)
    high = total.astype(BF16).astype(F32)
    lane = lax.broadcasted_iota(jnp.int32, (rows, 128), 1)
    out_ref[:, width:] = jnp.where(lane < 64, high, total - high).astype(BF16)
    block = 512
    for j in range(width // block):
        part = slice(j * block, (j + 1) * block)
        out_ref[:, part] = mm(pre_ref[...], w_ref[part, : 2 * ff], NT).astype(BF16)


def combine_kernel(back_ref, column_ref, gate_ref, out_ref, gate_out_ref):
    rows = back_ref.shape[0]
    tokens, width = out_ref.shape
    place = lax.broadcasted_iota(jnp.int32, (tokens, rows), 1)
    picks = [(place == column_ref[:, k : k + 1]).astype(F32) for k in range(2)]
    eye = (
        lax.broadcasted_iota(jnp.int32, (tokens, tokens), 0)
        == lax.broadcasted_iota(jnp.int32, (tokens, tokens), 1)
    ).astype(F32)
    for k in range(2):
        parts = mm(picks[k].astype(BF16), back_ref[:, width:])
        total = parts[:, 0:1] + parts[:, 64:65]
        total = jnp.sum(eye * total, axis=0, keepdims=True)
        gate_out_ref[k : k + 1, :] = (total / gate_ref[k : k + 1, :].astype(F32)).astype(BF16)
    pick = (picks[0] + picks[1]).astype(BF16)
    out_ref[...] = mm(pick, back_ref[:, :width]).astype(BF16)


def whole(shape, space=pltpu.VMEM):
    return pl.BlockSpec(shape, lambda *_: (0,) * len(shape), memory_space=space)


def call(kernel, outs, args, limit=60, **kw):
    return pl.pallas_call(
        kernel,
        out_shape=outs,
        compiler_params=pltpu.CompilerParams(vmem_limit_bytes=limit << 20),
        **kw,
    )(*args)


LONG = pl.CostEstimate(flops=1 << 40, bytes_accessed=1 << 30, transcendentals=0)


def ranked(values):
    return pl.pallas_call(
        lambda source, result: None,
        out_shape=jax.ShapeDtypeStruct(values.shape, values.dtype),
        in_specs=[pl.BlockSpec(memory_space=pl.ANY)],
        out_specs=pl.BlockSpec(memory_space=pl.ANY),
        input_output_aliases={0: 0},
        cost_estimate=LONG,
    )(values)


def on_device(moe_input, lm_grad, frame_grad, span_token, expert_ids, gate_weights, w_gate_up, w_down):
    tokens, width = moe_input.shape
    per_span = frame_grad.shape[0] // span_token.shape[0]
    experts = lax.axis_size("expert")
    n_seq = lax.axis_size("seq")
    cap = 2 * tokens * expert_ids.shape[1] // experts
    rows = experts * cap
    ff = w_down.shape[2]
    sds = jax.ShapeDtypeStruct

    def exchange(values):
        return lax.all_to_all(
            values.reshape(experts, cap, -1), "expert", split_axis=0, concat_axis=0, tiled=True
        ).reshape(rows, -1)

    names = jnp.repeat(span_token, per_span)[:, None]
    coded = jnp.concatenate([names // 32, names % 32], axis=1).astype(BF16)
    frames = jnp.concatenate([frame_grad, jnp.pad(coded, ((0, 0), (0, 126)))], axis=1)
    frames = lax.all_gather(frames, "seq", axis=0, tiled=True)

    gates = gate_weights.T
    send_input, target = call(
        functools.partial(route_kernel, experts, cap),
        (sds((rows, width), BF16), sds((2, tokens), jnp.int32)),
        (expert_ids.T, moe_input),
    )
    got_input = ranked(exchange(send_input))

    w_gate_up, w_down, target = lax.optimization_barrier((w_gate_up, w_down, target))
    weights = jnp.concatenate([w_gate_up.reshape(-1, 2 * ff), w_down[0]], axis=1)
    weights = lax.all_gather(weights, ("seq", "dp"), axis=0, tiled=True)

    own = (lax.axis_index("seq") * tokens).reshape(1)
    send_grad = call(
        upstream_kernel,
        sds((rows, width), BF16),
        (own, frames, lm_grad, target, gates),
        in_specs=[pl.BlockSpec(memory_space=pltpu.SMEM)]
        + [pl.BlockSpec(memory_space=pltpu.VMEM)] * 4,
    )
    got_grad = exchange(send_grad)

    hidden, gate_term, up_term = call(
        functools.partial(forward_kernel, ff),
        (sds((rows, ff), BF16), sds((rows, ff), F32), sds((rows, ff), F32)),
        (got_input, weights),
    )
    input_grad, pre_grad = call(
        functools.partial(backward_kernel, ff),
        (sds((rows, width + 128), BF16), sds((rows, 2 * ff), BF16)),
        (got_grad, weights, hidden, gate_term, up_term),
    )
    back = exchange(input_grad)

    partial = lax.dot_general(
        got_input, pre_grad, (((0,), (0,)), ((), ())), preferred_element_type=F32
    ).astype(BF16)
    partial = partial.reshape(n_seq, 2, -1, 2 * ff)
    core = lax.axis_index("dp")
    mine = lax.dynamic_index_in_dim(partial, core, 1, keepdims=False)
    other = lax.dynamic_index_in_dim(partial, 1 - core, 1, keepdims=False)
    other = lax.ppermute(other, "dp", [(0, 1), (1, 0)])
    pair = (mine.astype(F32) + other.astype(F32)).astype(BF16)
    grad = lax.psum_scatter(pair, "seq", scatter_dimension=0, tiled=True).astype(F32)
    grad_gate_up = grad.reshape(1, -1, 2, ff)

    grad_input, grad_gates = call(
        combine_kernel,
        (sds((tokens, width), BF16), sds((2, tokens), BF16)),
        (back, target.T, gates),
        cost_estimate=LONG,
    )
    return grad_input, grad_gates.T, grad_gate_up


def solution(mesh):
    every = ("expert", "seq", "dp")
    return jax.shard_map(
        on_device,
        mesh=mesh,
        in_specs=(
            P(every, None),
            P(every, None),
            P(every, None),
            P(every),
            P(every, None),
            P(every, None),
            P("expert", ("seq", "dp"), None, None),
            P("expert", ("seq", "dp"), None),
        ),
        out_specs=(P(every, None), P(every, None), P("expert", ("seq", "dp"), None, None)),
        check_vma=False,
    )
```

```python
import functools

import jax
import jax.numpy as jnp
from jax import lax
from jax.experimental import pallas as pl
from jax.experimental.pallas import tpu as pltpu
from jax.sharding import PartitionSpec as P

F32 = jnp.float32
BF16 = jnp.bfloat16
NX, NZ = 4, 8
NT = (((1,), (1,)), ((), ()))
NN = (((1,), (0,)), ((), ()))


def mm(a, b, dims=NN):
    return lax.dot_general(a, b, dims, preferred_element_type=F32)


def one_hot(target, rows):
    tokens = target.shape[1]
    return lax.broadcasted_iota(jnp.int32, (rows, tokens), 0) == target


def route_kernel(experts, cap, ids_ref, x_ref, out_ref, target_ref):
    tokens, width = x_ref.shape
    ids = ids_ref[...]
    members = [
        (lax.broadcasted_iota(jnp.int32, (experts, tokens), 0) == ids[k : k + 1]).astype(F32)
        for k in range(2)
    ]
    earlier = (
        lax.broadcasted_iota(jnp.int32, (tokens, tokens), 0)
        < lax.broadcasted_iota(jnp.int32, (tokens, tokens), 1)
    ).astype(F32)
    count = mm((members[0] + members[1]).astype(BF16), earlier.astype(BF16))
    line = lax.broadcasted_iota(jnp.int32, (128, tokens), 0)
    coded = jnp.zeros((128, tokens), F32)
    for k in range(2):
        position = jnp.sum(members[k] * count, axis=0, keepdims=True)
        target_ref[k : k + 1, :] = ids[k : k + 1] * cap + position.astype(jnp.int32)
        coded = jnp.where(line == 2 * k, ids[k : k + 1].astype(F32), coded)
        coded = jnp.where(line == 2 * k + 1, position, coded)
    out_ref[:, :width] = x_ref[...]
    out_ref[:, width:] = coded.T.astype(BF16)


def pack_kernel(cap, place_ref, *refs):
    blocks, outs = refs[:9], refs[9:]
    width = outs[0].shape[1]
    my_x, my_z = place_ref[0], place_ref[1]

    def pick(block, shift):
        codes = block[:, width:].astype(F32).T.astype(jnp.int32)
        tokens = codes.shape[1]
        rows = lax.broadcasted_iota(jnp.int32, (NX * cap, tokens), 0)
        select = jnp.zeros((NX * cap, tokens), F32)
        for k in range(2):
            expert, position = codes[2 * k : 2 * k + 1], codes[2 * k + 1 : 2 * k + 2]
            away = (expert // NZ - my_x + NX) % NX
            row = jnp.where(expert % NZ == my_z, away * cap + position, -1)
            select += (rows == row).astype(F32)
        picked = mm(select.astype(BF16), block[:, :width]).astype(BF16)
        first = pl.multiple_of(((my_z + shift) % NZ) * cap, cap)
        for d in range(NX):
            outs[d][pl.ds(first, cap), :] = picked[d * cap : (d + 1) * cap]

    for block, shift in zip(blocks[:7], (0, 7, 6, 5, 1, 2, 3)):
        pick(block[...], shift)
    pick(jnp.concatenate([blocks[7][...], blocks[8][...]], axis=0), 4)


def upstream_kernel(own_ref, frames_ref, lm_ref, target_ref, gate_ref, send_ref):
    tokens, width = lm_ref.shape
    frames = frames_ref.shape[0]
    coded = frames_ref[:, width:].astype(F32)
    name = (coded[:, 0:1] * 32.0 + coded[:, 1:2]).astype(jnp.int32) - own_ref[0]
    named = (lax.broadcasted_iota(jnp.int32, (frames, tokens), 1) == name).astype(F32)
    cond = mm(named.T.astype(BF16), frames_ref[:, :width])
    upstream = (lm_ref[...].astype(F32) + cond).astype(BF16)
    rows = send_ref.shape[0]
    hot = [one_hot(target_ref[k : k + 1, :], rows).astype(F32) for k in range(2)]
    gates = gate_ref[...].astype(F32)
    gate = jnp.sum(hot[0] * gates[0:1] + hot[1] * gates[1:2], axis=1, keepdims=True)
    send_ref[...] = (mm((hot[0] + hot[1]).astype(BF16), upstream) * gate).astype(BF16)


def forward_kernel(
    ff, place_ref, x0, x1, x2, x3, w_ref, hidden_ref, gate_term_ref, up_term_ref, mine_ref, other_ref
):
    rows, width = x0.shape
    core = place_ref[2]
    for d, x_ref in enumerate((x0, x1, x2, x3)):
        first = pl.multiple_of(((place_ref[0] + NX - d) % NX) * rows, rows)
        at = pl.ds(first, rows)
        for j in range(width // 256):
            own = pl.ds(pl.multiple_of((2 * j + core) * 128, 128), 128)
            away = pl.ds(pl.multiple_of((2 * j + 1 - core) * 128, 128), 128)
            mine_ref[at, j * 128 : (j + 1) * 128] = x_ref[:, own]
            other_ref[at, j * 128 : (j + 1) * 128] = x_ref[:, away]
        pre = mm(x_ref[...], w_ref[:, : 2 * ff])
        gate_pre = pre[:, :ff]
        up_pre = pre[:, ff:]
        sig = jax.nn.sigmoid(gate_pre)
        activated = gate_pre * sig
        slope = sig * (1.0 + gate_pre * (1.0 - sig))
        hidden_ref[at, :] = (activated * up_pre).astype(BF16)
        gate_term_ref[at, :] = up_pre * slope
        up_term_ref[at, :] = activated


def backward_kernel(
    ff, y_any, w_any, hidden_any, gate_any, up_any, out_any, pre_ref,
    y, wd, wg, hidden, gate_term, up_term, out, extra, sems,
):
    rows, width = y.shape
    half, block = width // 2, width // 4
    copies = []

    def fetch(source, target):
        copies.append(pltpu.make_async_copy(source, target, sems.at[len(copies)]))
        copies[-1].start()

    for h in range(2):
        part = slice(h * half, (h + 1) * half)
        fetch(y_any.at[:, part], y.at[:, part])
        fetch(w_any.at[part, 2 * ff :], wd.at[part, :])
    fetch(gate_any, gate_term)
    fetch(up_any, up_term)
    fetch(hidden_any, hidden)
    for j in range(4):
        part = slice(j * block, (j + 1) * block)
        fetch(w_any.at[part, : 2 * ff], wg.at[part, :])
    copies[0].wait()
    copies[1].wait()
    hidden_grad = mm(y[:, :half], wd[:half, :])
    copies[2].wait()
    copies[3].wait()
    hidden_grad += mm(y[:, half:], wd[half:, :])
    copies[4].wait()
    pre_ref[:, :ff] = (hidden_grad * gate_term[...]).astype(BF16)
    copies[5].wait()
    pre_ref[:, ff:] = (hidden_grad * up_term[...]).astype(BF16)
    copies[6].wait()
    total = jnp.sum(hidden[...].astype(F32) * hidden_grad, axis=1, keepdims=True)
    high = total.astype(BF16).astype(F32)
    lane = lax.broadcasted_iota(jnp.int32, (rows, 128), 1)
    extra[...] = jnp.where(lane < 64, high, total - high).astype(BF16)
    fetch(extra, out_any.at[:, width:])
    for j in range(4):
        part = slice(j * block, (j + 1) * block)
        copies[7 + j].wait()
        out[:, part] = mm(pre_ref[...], wg[part, :], NT).astype(BF16)
        fetch(out.at[:, part], out_any.at[:, part])
    for j in range(5):
        copies[11 + j].wait()


def combine_kernel(back_ref, column_ref, gate_ref, out_ref, gate_out_ref):
    rows = back_ref.shape[0]
    tokens, width = out_ref.shape
    place = lax.broadcasted_iota(jnp.int32, (tokens, rows), 1)
    picks = [(place == column_ref[:, k : k + 1]).astype(F32) for k in range(2)]
    eye = (
        lax.broadcasted_iota(jnp.int32, (tokens, tokens), 0)
        == lax.broadcasted_iota(jnp.int32, (tokens, tokens), 1)
    ).astype(F32)
    for k in range(2):
        parts = mm(picks[k].astype(BF16), back_ref[:, width:])
        total = parts[:, 0:1] + parts[:, 64:65]
        total = jnp.sum(eye * total, axis=0, keepdims=True)
        gate_out_ref[k : k + 1, :] = (total / gate_ref[k : k + 1, :].astype(F32)).astype(BF16)
    pick = (picks[0] + picks[1]).astype(BF16)
    out_ref[...] = mm(pick, back_ref[:, :width]).astype(BF16)


def call(kernel, outs, args, limit=60, **kw):
    return pl.pallas_call(
        kernel,
        out_shape=outs,
        compiler_params=pltpu.CompilerParams(vmem_limit_bytes=limit << 20),
        **kw,
    )(*args)


LONG = pl.CostEstimate(flops=1 << 40, bytes_accessed=1 << 30, transcendentals=0)


def along(dx, dz):
    return [
        (x * NZ + z, (x + dx) % NX * NZ + (z + dz) % NZ) for x in range(NX) for z in range(NZ)
    ]


def on_device(moe_input, lm_grad, frame_grad, span_token, expert_ids, gate_weights, w_gate_up, w_down):
    tokens, width = moe_input.shape
    per_span = frame_grad.shape[0] // span_token.shape[0]
    experts = NX * NZ
    cap = 2 * tokens * expert_ids.shape[1] // experts
    rows = experts * cap
    ff = w_down.shape[2]
    sds = jax.ShapeDtypeStruct
    me = lax.axis_index("expert")
    core = lax.axis_index("dp")
    place = jnp.stack([me // NZ, me % NZ, core]).astype(jnp.int32)
    smem = pl.BlockSpec(memory_space=pltpu.SMEM)
    vmem = pl.BlockSpec(memory_space=pltpu.VMEM)
    hbm = pl.BlockSpec(memory_space=pltpu.HBM)
    any_space = pl.BlockSpec(memory_space=pl.ANY)

    def exchange(values):
        return lax.all_to_all(
            values.reshape(experts, cap, -1), "expert", split_axis=0, concat_axis=0, tiled=True
        ).reshape(rows, -1)

    names = jnp.repeat(span_token, per_span)[:, None]
    coded = jnp.concatenate([names // 32, names % 32], axis=1).astype(BF16)
    frames = jnp.concatenate([frame_grad, jnp.pad(coded, ((0, 0), (0, 126)))], axis=1)
    frames = lax.all_gather(frames, "seq", axis=0, tiled=True)

    gates = gate_weights.T
    block, target = call(
        functools.partial(route_kernel, experts, cap),
        (sds((tokens, width + 128), BF16), sds((2, tokens), jnp.int32)),
        (expert_ids.T, moe_input),
    )
    up, down = [block], [block]
    for hop in range(3):
        ahead = lax.ppermute(up[-1], "expert", along(0, 1))
        behind = lax.ppermute(down[-1], "expert", along(0, -1))
        ahead, behind = lax.optimization_barrier((ahead, behind))
        up.append(ahead)
        down.append(behind)
    last_up = lax.ppermute(up[3][: tokens // 2], "expert", along(0, 1))
    last_down = lax.ppermute(down[3][tokens // 2 :], "expert", along(0, -1))

    w_gate_up, w_down, _ = lax.optimization_barrier((w_gate_up, w_down, up[1]))
    weights = jnp.concatenate([w_gate_up.reshape(-1, 2 * ff), w_down[0]], axis=1)
    weights = lax.all_gather(weights, ("seq", "dp"), axis=0, tiled=True)

    own = (lax.axis_index("seq") * tokens).reshape(1)
    lm_grad, _, _ = lax.optimization_barrier((lm_grad, up[3], down[3]))
    send_grad = call(
        upstream_kernel,
        sds((rows, width), BF16),
        (own, frames, lm_grad, target, gates),
        in_specs=[smem] + [vmem] * 4,
    )
    got_grad = exchange(send_grad)

    packed = call(
        functools.partial(pack_kernel, cap),
        [sds((NZ * cap, width), BF16)] * NX,
        (place, block, *up[1:], *down[1:], last_up, last_down),
        in_specs=[smem] + [vmem] * 9,
    )
    arrived = [packed[0]]
    for d in range(1, NX):
        arrived.append(lax.ppermute(packed[d], "expert", along(d, 0)))

    hidden, gate_term, up_term, x_mine, x_other = call(
        functools.partial(forward_kernel, ff),
        (
            sds((rows, ff), BF16), sds((rows, ff), F32), sds((rows, ff), F32),
            sds((rows, width // 2), BF16), sds((rows, width // 2), BF16),
        ),
        (place, *arrived, weights),
        in_specs=[smem] + [vmem] * 5,
    )
    input_grad, pre_grad = call(
        functools.partial(backward_kernel, ff),
        (sds((rows, width + 128), BF16), sds((rows, 2 * ff), BF16)),
        (got_grad, weights, hidden, gate_term, up_term),
        in_specs=[any_space] + [hbm] * 4,
        out_specs=[hbm, vmem],
        scratch_shapes=[
            pltpu.VMEM((rows, width), BF16),
            pltpu.VMEM((width, ff), BF16),
            pltpu.VMEM((width, 2 * ff), BF16),
            pltpu.VMEM((rows, ff), BF16),
            pltpu.VMEM((rows, ff), F32),
            pltpu.VMEM((rows, ff), F32),
            pltpu.VMEM((rows, width), BF16),
            pltpu.VMEM((rows, 128), BF16),
            pltpu.SemaphoreType.DMA((16,)),
        ],
    )
    back = exchange(input_grad)

    rows_first = (((0,), (0,)), ((), ()))
    other = mm(x_other, pre_grad, rows_first).astype(BF16)
    other = lax.ppermute(other, "dp", [(0, 1), (1, 0)])
    pair = (mm(x_mine, pre_grad, rows_first) + other.astype(F32)).astype(BF16)
    grad = lax.psum_scatter(pair, "seq", scatter_dimension=0, tiled=True).astype(F32)
    grad_gate_up = grad.reshape(1, -1, 2, ff)

    grad_input, grad_gates = call(
        combine_kernel,
        (sds((tokens, width), BF16), sds((2, tokens), BF16)),
        (back, target.T, gates),
        limit=20,
        cost_estimate=LONG,
    )
    return grad_input, grad_gates.T, grad_gate_up


def solution(mesh):
    every = ("expert", "seq", "dp")
    return jax.shard_map(
        on_device,
        mesh=mesh,
        in_specs=(
            P(every, None),
            P(every, None),
            P(every, None),
            P(every),
            P(every, None),
            P(every, None),
            P("expert", ("seq", "dp"), None, None),
            P("expert", ("seq", "dp"), None),
        ),
        out_specs=(P(every, None), P(every, None), P("expert", ("seq", "dp"), None, None)),
        check_vma=False,
    )
```

```python
import functools

import jax
import jax.numpy as jnp
from jax import lax
from jax.experimental import pallas as pl
from jax.experimental.pallas import tpu as pltpu
from jax.sharding import PartitionSpec as P

F32 = jnp.float32
BF16 = jnp.bfloat16
NT = (((1,), (1,)), ((), ()))
NN = (((1,), (0,)), ((), ()))
TN = (((0,), (0,)), ((), ()))


def mm(a, b, dims=NN):
    return lax.dot_general(a, b, dims, preferred_element_type=F32)


def one_hot(target, rows):
    tokens = target.shape[1]
    return lax.broadcasted_iota(jnp.int32, (rows, tokens), 0) == target


def route_kernel(experts, cap, ids_ref, x_any, send_any, target_ref, x, send, sems):
    load = pltpu.make_async_copy(x_any, x, sems.at[0])
    load.start()
    tokens = ids_ref.shape[1]
    ids = ids_ref[...]
    members = [
        (lax.broadcasted_iota(jnp.int32, (experts, tokens), 0) == ids[k : k + 1]).astype(F32)
        for k in range(2)
    ]
    earlier = (
        lax.broadcasted_iota(jnp.int32, (tokens, tokens), 0)
        < lax.broadcasted_iota(jnp.int32, (tokens, tokens), 1)
    ).astype(F32)
    count = mm((members[0] + members[1]).astype(BF16), earlier.astype(BF16))
    rows = experts * cap
    targets = []
    for k in range(2):
        position = jnp.sum(members[k] * count, axis=0, keepdims=True).astype(jnp.int32)
        targets.append(ids[k : k + 1] * cap + position)
        target_ref[k : k + 1, :] = targets[k]
    load.wait()
    block = rows // 4
    stores = []
    for j in range(4):
        part = slice(j * block, (j + 1) * block)
        select = sum(one_hot(t - j * block, block).astype(F32) for t in targets)
        send[part, :] = mm(select.astype(BF16), x[...]).astype(BF16)
        stores.append(pltpu.make_async_copy(send.at[part, :], send_any.at[part, :], sems.at[1 + j]))
        stores[j].start()
    for store in stores:
        store.wait()


def upstream_kernel(own_ref, names_ref, frames_ref, lm_ref, target_ref, gate_ref, send_ref):
    tokens = lm_ref.shape[0]
    frames = frames_ref.shape[0]
    own = lax.broadcasted_iota(jnp.int32, (tokens, frames), 0) + own_ref[0]
    named = (own == names_ref[...]).astype(F32)
    cond = mm(named.astype(BF16), frames_ref[...])
    upstream = (lm_ref[...].astype(F32) + cond).astype(BF16)
    rows = send_ref.shape[0]
    hot = [one_hot(target_ref[k : k + 1, :], rows).astype(F32) for k in range(2)]
    gates = gate_ref[...].astype(F32)
    gate = jnp.sum(hot[0] * gates[0:1] + hot[1] * gates[1:2], axis=1, keepdims=True)
    send_ref[...] = (mm((hot[0] + hot[1]).astype(BF16), upstream) * gate).astype(BF16)


def forward_kernel(
    ff, n_seq, place_ref, x_ref, w_ref, hidden_ref, gate_term_ref, up_term_ref, mine_ref, other_ref
):
    seq, core = place_ref[0], place_ref[1]
    for j in range(n_seq):
        owner = (seq + j) % n_seq
        own = pl.ds(pl.multiple_of((2 * owner + core) * 128, 128), 128)
        away = pl.ds(pl.multiple_of((2 * owner + 1 - core) * 128, 128), 128)
        mine_ref[:, j * 128 : (j + 1) * 128] = x_ref[:, own]
        other_ref[:, j * 128 : (j + 1) * 128] = x_ref[:, away]
    pre = mm(x_ref[...], w_ref[:, : 2 * ff])
    gate_pre = pre[:, :ff]
    up_pre = pre[:, ff:]
    sig = jax.nn.sigmoid(gate_pre)
    activated = gate_pre * sig
    slope = sig * (1.0 + gate_pre * (1.0 - sig))
    hidden_ref[...] = (activated * up_pre).astype(BF16)
    gate_term_ref[...] = up_pre * slope
    up_term_ref[...] = activated


def backward_kernel(
    ff, y_any, w_any, hidden_any, gate_any, up_any, out_any, pre_ref,
    y, wd, wg, hidden, gate_term, up_term, out, extra, sems,
):
    rows, width = y.shape
    half, block = width // 2, width // 4
    copies = []

    def fetch(source, target):
        copies.append(pltpu.make_async_copy(source, target, sems.at[len(copies)]))
        copies[-1].start()

    for h in range(2):
        part = slice(h * half, (h + 1) * half)
        fetch(y_any.at[:, part], y.at[:, part])
        fetch(w_any.at[part, 2 * ff :], wd.at[part, :])
    copies[0].wait()
    copies[1].wait()
    fetch(gate_any, gate_term)
    fetch(up_any, up_term)
    fetch(hidden_any, hidden)
    hidden_grad = mm(y[:, :half], wd[:half, :])
    copies[2].wait()
    copies[3].wait()
    for j in range(4):
        part = slice(j * block, (j + 1) * block)
        fetch(w_any.at[part, : 2 * ff], wg.at[part, :])
    hidden_grad += mm(y[:, half:], wd[half:, :])
    copies[4].wait()
    pre_ref[:, :ff] = (hidden_grad * gate_term[...]).astype(BF16)
    copies[5].wait()
    pre_ref[:, ff:] = (hidden_grad * up_term[...]).astype(BF16)
    copies[6].wait()
    total = jnp.sum(hidden[...].astype(F32) * hidden_grad, axis=1, keepdims=True)
    high = total.astype(BF16).astype(F32)
    lane = lax.broadcasted_iota(jnp.int32, (rows, 128), 1)
    extra[...] = jnp.where(lane < 64, high, total - high).astype(BF16)
    fetch(extra, out_any.at[:, width:])
    for j in range(4):
        part = slice(j * block, (j + 1) * block)
        copies[7 + j].wait()
        out[:, part] = mm(pre_ref[...], wg[part, :], NT).astype(BF16)
        fetch(out.at[:, part], out_any.at[:, part])
    for j in range(5):
        copies[11 + j].wait()


def away_kernel(x_ref, pre_ref, out_ref):
    out_ref[...] = mm(x_ref[...], pre_ref[...], TN).astype(BF16)


def near_kernel(x_any, pre_any, other_any, *refs):
    count = len(refs) - 4
    outs, (x, pre, other, sems) = refs[:count], refs[count:]
    rows = x.shape[1] // count
    copies = [pltpu.make_async_copy(pre_any, pre, sems.at[0])]
    copies[0].start()
    loads = []
    for j in range(count):
        part = slice(j * rows, (j + 1) * rows)
        loads.append(
            (
                pltpu.make_async_copy(x_any.at[:, part], x.at[:, part], sems.at[1 + 2 * j]),
                pltpu.make_async_copy(other_any.at[part, :], other.at[part, :], sems.at[2 + 2 * j]),
            )
        )
        for load in loads[j]:
            load.start()
    copies[0].wait()
    stores = []
    for j in range(count):
        part = slice(j * rows, (j + 1) * rows)
        for load in loads[j]:
            load.wait()
        both = mm(x[:, part], pre[...], TN) + other[part, :].astype(F32)
        other[part, :] = both.astype(BF16)
        stores.append(
            pltpu.make_async_copy(other.at[part, :], outs[j], sems.at[1 + 2 * count + j])
        )
        stores[j].start()
    for store in stores:
        store.wait()


def total_kernel(*refs):
    total = refs[0][...].astype(F32)
    for ref in refs[1:-1]:
        total += ref[...].astype(F32)
    ff = total.shape[1] // 2
    refs[-1][:, 0, :] = total[:, :ff]
    refs[-1][:, 1, :] = total[:, ff:]


def combine_kernel(back_any, column_ref, gate_ref, out_ref, gate_out_ref, back, sems):
    rows = back.shape[0]
    tokens, width = out_ref.shape
    block = rows // 4
    loads = []
    for j in range(4):
        part = slice(j * block, (j + 1) * block)
        loads.append(pltpu.make_async_copy(back_any.at[part, :], back.at[part, :], sems.at[j]))
        loads[j].start()
    place = lax.broadcasted_iota(jnp.int32, (tokens, rows), 1)
    picks = [(place == column_ref[:, k : k + 1]).astype(F32) for k in range(2)]
    pick = (picks[0] + picks[1]).astype(BF16)
    total = None
    for j in range(4):
        part = slice(j * block, (j + 1) * block)
        loads[j].wait()
        term = mm(pick[:, part], back[part, :width])
        total = term if total is None else total + term
    out_ref[...] = total.astype(BF16)
    eye = (
        lax.broadcasted_iota(jnp.int32, (tokens, tokens), 0)
        == lax.broadcasted_iota(jnp.int32, (tokens, tokens), 1)
    ).astype(F32)
    for k in range(2):
        parts = mm(picks[k].astype(BF16), back[:, width:])
        gate = jnp.sum(eye * (parts[:, 0:1] + parts[:, 64:65]), axis=0, keepdims=True)
        gate_out_ref[k : k + 1, :] = (gate / gate_ref[k : k + 1, :].astype(F32)).astype(BF16)


def call(kernel, outs, args, limit=60, **kw):
    return pl.pallas_call(
        kernel,
        out_shape=outs,
        compiler_params=pltpu.CompilerParams(vmem_limit_bytes=limit << 20),
        **kw,
    )(*args)


LONG = pl.CostEstimate(flops=1 << 40, bytes_accessed=1 << 30, transcendentals=0)


def ranked(values):
    return pl.pallas_call(
        lambda source, result: None,
        out_shape=jax.ShapeDtypeStruct(values.shape, values.dtype),
        in_specs=[pl.BlockSpec(memory_space=pl.ANY)],
        out_specs=pl.BlockSpec(memory_space=pl.ANY),
        input_output_aliases={0: 0},
        compiler_params=pltpu.CompilerParams(vmem_limit_bytes=1 << 20),
        cost_estimate=LONG,
    )(values)


def on_device(moe_input, lm_grad, frame_grad, span_token, expert_ids, gate_weights, w_gate_up, w_down):
    tokens, width = moe_input.shape
    per_span = frame_grad.shape[0] // span_token.shape[0]
    experts = lax.axis_size("expert")
    n_seq = lax.axis_size("seq")
    cap = 2 * tokens * expert_ids.shape[1] // experts
    rows = experts * cap
    ff = w_down.shape[2]
    sds = jax.ShapeDtypeStruct
    any_space = pl.BlockSpec(memory_space=pl.ANY)
    vmem = pl.BlockSpec(memory_space=pltpu.VMEM)
    smem = pl.BlockSpec(memory_space=pltpu.SMEM)

    def exchange(values):
        return lax.all_to_all(
            values.reshape(experts, cap, -1), "expert", split_axis=0, concat_axis=0, tiled=True
        ).reshape(rows, -1)

    seq = lax.axis_index("seq")
    place = jnp.stack([seq, lax.axis_index("dp")]).astype(jnp.int32)
    frames = lax.all_gather(frame_grad, "seq", axis=0, tiled=True)

    gates = gate_weights.T
    send_input, target = call(
        functools.partial(route_kernel, experts, cap),
        (sds((rows, width), BF16), sds((2, tokens), jnp.int32)),
        (expert_ids.T, moe_input),
        in_specs=[vmem, any_space],
        out_specs=[any_space, vmem],
        scratch_shapes=[
            pltpu.VMEM((tokens, width), BF16),
            pltpu.VMEM((rows, width), BF16),
            pltpu.SemaphoreType.DMA((5,)),
        ],
    )
    got_input = ranked(exchange(send_input))

    w_gate_up, w_down, target = lax.optimization_barrier((w_gate_up, w_down, target))
    weights = jnp.concatenate([w_gate_up.reshape(-1, 2 * ff), w_down[0]], axis=1)
    weights = lax.all_gather(weights, ("seq", "dp"), axis=0, tiled=True)

    span_token, _ = lax.optimization_barrier((span_token, target))
    names = lax.all_gather(span_token, "seq", axis=0, tiled=True)
    names = jnp.repeat(names, per_span)[None, :]
    send_grad = call(
        upstream_kernel,
        sds((rows, width), BF16),
        ((seq * tokens).reshape(1), names, frames, lm_grad, target, gates),
        in_specs=[smem] + [vmem] * 5,
        cost_estimate=LONG,
    )
    got_grad = exchange(send_grad)

    hidden, gate_term, up_term, x_mine, x_other = call(
        functools.partial(forward_kernel, ff, n_seq),
        (
            sds((rows, ff), BF16), sds((rows, ff), F32), sds((rows, ff), F32),
            sds((rows, width // 2), BF16), sds((rows, width // 2), BF16),
        ),
        (place, got_input, weights),
        in_specs=[smem, vmem, vmem],
    )
    input_grad, pre_grad = call(
        functools.partial(backward_kernel, ff),
        (sds((rows, width + 128), BF16), sds((rows, 2 * ff), BF16)),
        (got_grad, weights, hidden, gate_term, up_term),
        limit=60,
        in_specs=[any_space] * 5,
        out_specs=[any_space, pl.BlockSpec(memory_space=pltpu.VMEM)],
        scratch_shapes=[
            pltpu.VMEM((rows, width), BF16),
            pltpu.VMEM((width, ff), BF16),
            pltpu.VMEM((width, 2 * ff), BF16),
            pltpu.VMEM((rows, ff), BF16),
            pltpu.VMEM((rows, ff), F32),
            pltpu.VMEM((rows, ff), F32),
            pltpu.VMEM((rows, width), BF16),
            pltpu.VMEM((rows, 128), BF16),
            pltpu.SemaphoreType.DMA((16,)),
        ],
    )
    back = exchange(input_grad)

    other = call(
        away_kernel,
        sds((width // 2, 2 * ff), BF16),
        (x_other, pre_grad),
        grid=(4,),
        in_specs=[
            pl.BlockSpec((rows, width // 8), lambda j: (0, j)),
            pl.BlockSpec((rows, 2 * ff), lambda j: (0, 0)),
        ],
        out_specs=pl.BlockSpec((width // 8, 2 * ff), lambda j: (j, 0)),
    )
    other = lax.ppermute(other, "dp", [(0, 1), (1, 0)])
    sums = call(
        near_kernel,
        [sds((width // 2 // n_seq, 2 * ff), BF16)] * n_seq,
        (x_mine, pre_grad, other),
        in_specs=[any_space] * 3,
        out_specs=[any_space] * n_seq,
        scratch_shapes=[
            pltpu.VMEM((rows, width // 2), BF16),
            pltpu.VMEM((rows, 2 * ff), BF16),
            pltpu.VMEM((width // 2, 2 * ff), BF16),
            pltpu.SemaphoreType.DMA((1 + 3 * n_seq,)),
        ],
    )
    shares = [sums[0]]
    for d in range(1, n_seq):
        pairs = [(i, (i + d) % n_seq) for i in range(n_seq)]
        shares.append(lax.ppermute(sums[d], "seq", pairs))
    grad_gate_up = call(
        total_kernel, sds((width // 2 // n_seq, 2, ff), F32), shares, limit=20
    )[None]

    grad_input, grad_gates = call(
        combine_kernel,
        (sds((tokens, width), BF16), sds((2, tokens), BF16)),
        (back, target.T, gates),
        limit=20,
        in_specs=[any_space, vmem, vmem],
        out_specs=[vmem, vmem],
        scratch_shapes=[
            pltpu.VMEM((rows, width + 128), BF16),
            pltpu.SemaphoreType.DMA((4,)),
        ],
        cost_estimate=LONG,
    )
    return grad_input, grad_gates.T, grad_gate_up


def solution(mesh):
    every = ("expert", "seq", "dp")
    return jax.shard_map(
        on_device,
        mesh=mesh,
        in_specs=(
            P(every, None),
            P(every, None),
            P(every, None),
            P(every),
            P(every, None),
            P(every, None),
            P("expert", ("seq", "dp"), None, None),
            P("expert", ("seq", "dp"), None),
        ),
        out_specs=(P(every, None), P(every, None), P("expert", ("seq", "dp"), None, None)),
        check_vma=False,
    )
```

```python
import functools

import jax
import jax.numpy as jnp
from jax import lax
from jax.experimental import pallas as pl
from jax.experimental.pallas import tpu as pltpu
from jax.sharding import PartitionSpec as P

F32 = jnp.float32
BF16 = jnp.bfloat16
NT = (((1,), (1,)), ((), ()))
NN = (((1,), (0,)), ((), ()))
TN = (((0,), (0,)), ((), ()))


def mm(a, b, dims=NN):
    return lax.dot_general(a, b, dims, preferred_element_type=F32)


def one_hot(target, rows):
    tokens = target.shape[1]
    return lax.broadcasted_iota(jnp.int32, (rows, tokens), 0) == target


def route_kernel(experts, cap, ids_ref, x_any, send_any, target_ref, x, send, sems):
    load = pltpu.make_async_copy(x_any, x, sems.at[0])
    load.start()
    tokens, width = x.shape
    ids = ids_ref[...]
    members = [
        (lax.broadcasted_iota(jnp.int32, (experts, tokens), 0) == ids[k : k + 1]).astype(F32)
        for k in range(2)
    ]
    earlier = (
        lax.broadcasted_iota(jnp.int32, (tokens, tokens), 0)
        < lax.broadcasted_iota(jnp.int32, (tokens, tokens), 1)
    ).astype(F32)
    count = mm((members[0] + members[1]).astype(BF16), earlier.astype(BF16))
    half = experts * cap // 2
    sub = cap // 2
    targets = []
    for k in range(2):
        position = jnp.sum(members[k] * count, axis=0, keepdims=True).astype(jnp.int32)
        low = jnp.where(position < sub, position, position + (half - sub))
        targets.append(ids[k : k + 1] * sub + low)
        target_ref[k : k + 1, :] = targets[k]
    load.wait()
    block = half // 2
    stores = []
    for j in range(4):
        select = sum(one_hot(t - j * block, block).astype(F32) for t in targets)
        to = (slice(j % 2 * block, (j % 2 + 1) * block), slice(j // 2 * width, (j // 2 + 1) * width))
        send[to] = mm(select.astype(BF16), x[...]).astype(BF16)
        stores.append(pltpu.make_async_copy(send.at[to], send_any.at[to], sems.at[1 + j]))
        stores[j].start()
    for store in stores:
        store.wait()


def upstream_kernel(own_ref, names_ref, frames_ref, lm_ref, target_ref, gate_ref, send_ref):
    tokens = lm_ref.shape[0]
    frames = frames_ref.shape[0]
    own = lax.broadcasted_iota(jnp.int32, (tokens, frames), 0) + own_ref[0]
    named = (own == names_ref[...]).astype(F32)
    cond = mm(named.astype(BF16), frames_ref[...])
    upstream = (lm_ref[...].astype(F32) + cond).astype(BF16)
    half, width = send_ref.shape[0], lm_ref.shape[1]
    hot = [one_hot(target_ref[k : k + 1, :], 2 * half).astype(F32) for k in range(2)]
    gates = gate_ref[...].astype(F32)
    gate = jnp.sum(hot[0] * gates[0:1] + hot[1] * gates[1:2], axis=1, keepdims=True)
    scaled = (mm((hot[0] + hot[1]).astype(BF16), upstream) * gate).astype(BF16)
    send_ref[:, :width] = scaled[:half]
    send_ref[:, width:] = scaled[half:]


def forward_kernel(
    ff, place_ref, x_ref, w_ref, hidden_ref, gate_term_ref, up_term_ref, columns_ref, *keep
):
    half, width = x_ref.shape[0], x_ref.shape[1] // 2
    core = place_ref[1]
    for i in range(2):
        at = slice(i * half, (i + 1) * half)
        for j in range(width // 256):
            own = pl.ds(pl.multiple_of(i * width + (2 * j + core) * 128, 128), 128)
            away = pl.ds(pl.multiple_of(i * width + (2 * j + 1 - core) * 128, 128), 128)
            columns_ref[at, j * 128 : (j + 1) * 128] = x_ref[:, away]
            columns_ref[at, width // 2 + j * 128 : width // 2 + (j + 1) * 128] = x_ref[:, own]
        pre = mm(x_ref[:, i * width : (i + 1) * width], w_ref[:, : 2 * ff])
        gate_pre = pre[:, :ff]
        up_pre = pre[:, ff:]
        sig = jax.nn.sigmoid(gate_pre)
        activated = gate_pre * sig
        slope = sig * (1.0 + gate_pre * (1.0 - sig))
        hidden_ref[at, :] = (activated * up_pre).astype(BF16)
        gate_term_ref[at, :] = up_pre * slope
        up_term_ref[at, :] = activated
    for ref in keep:
        ref[...] = w_ref[...]


def backward_kernel(
    ff, y_any, w_any, hidden_any, gate_any, up_any, out_any, pre_any,
    y, wd, wg, hidden, gate_term, up_term, out, pre, sems,
):
    half, width = y_any.shape[0], y_any.shape[1] // 2
    chunk = width // 4
    copies = []

    def fetch(source, target):
        copies.append(pltpu.make_async_copy(source, target, sems.at[len(copies)]))
        copies[-1].start()

    for c in range(4):
        part = slice(c * chunk, (c + 1) * chunk)
        fetch(w_any.at[part, 2 * ff :], wd.at[part, :])
        for i in range(2):
            begin = i * width + c * chunk
            fetch(y_any.at[:, begin : begin + chunk], y.at[i * half : (i + 1) * half, part])
    hidden_grad = None
    for c in range(4):
        part = slice(c * chunk, (c + 1) * chunk)
        for n in range(3):
            copies[3 * c + n].wait()
        if c == 0:
            fetch(gate_any, gate_term)
            fetch(up_any, up_term)
            fetch(hidden_any, hidden)
        if c == 1:
            for j in range(4):
                to = slice(j * chunk, (j + 1) * chunk)
                fetch(w_any.at[to, : 2 * ff], wg.at[to, :])
        term = mm(y[:, part], wd[part, :])
        hidden_grad = term if hidden_grad is None else hidden_grad + term
    for n in range(12, 19):
        copies[n].wait()
    extra = jnp.zeros((half, 128), F32)
    lane = lax.broadcasted_iota(jnp.int32, (half, 128), 1)
    for i in range(2):
        at = slice(i * half, (i + 1) * half)
        grad = hidden_grad[at]
        pre[at, :ff] = (grad * gate_term[at, :]).astype(BF16)
        pre[at, ff:] = (grad * up_term[at, :]).astype(BF16)
        total = jnp.sum(hidden[at, :].astype(F32) * grad, axis=1, keepdims=True)
        high = total.astype(BF16).astype(F32)
        extra = jnp.where(lane // 64 == i, jnp.where(lane % 64 < 32, high, total - high), extra)
    out[:, 2 * width :] = extra.astype(BF16)
    fetch(out.at[:, 2 * width :], out_any.at[:, 2 * width :])
    for j in range(4):
        grads = mm(pre[...], wg[j * chunk : (j + 1) * chunk, :], NT).astype(BF16)
        for i in range(2):
            to = slice(i * width + j * chunk, i * width + (j + 1) * chunk)
            out[:, to] = grads[i * half : (i + 1) * half]
            fetch(out.at[:, to], out_any.at[:, to])
    fetch(pre, pre_any)
    for copy in copies[19:]:
        copy.wait()

def combine_kernel(back_any, column_ref, gate_ref, out_ref, gate_out_ref, back, sems):
    half = back.shape[0]
    tokens, width = out_ref.shape
    loads = []
    for i, part in enumerate((slice(0, width), slice(width, 2 * width + 128))):
        loads.append(pltpu.make_async_copy(back_any.at[:, part], back.at[:, part], sems.at[i]))
        loads[i].start()
    place = lax.broadcasted_iota(jnp.int32, (tokens, 2 * half), 1)
    picks = [(place == column_ref[:, k : k + 1]).astype(F32) for k in range(2)]
    pick = (picks[0] + picks[1]).astype(BF16)
    loads[0].wait()
    total = mm(pick[:, :half], back[:, :width])
    loads[1].wait()
    total += mm(pick[:, half:], back[:, width : 2 * width])
    out_ref[...] = total.astype(BF16)
    eye = (
        lax.broadcasted_iota(jnp.int32, (tokens, tokens), 0)
        == lax.broadcasted_iota(jnp.int32, (tokens, tokens), 1)
    ).astype(F32)
    for k in range(2):
        first = mm(picks[k][:, :half].astype(BF16), back[:, 2 * width :])
        second = mm(picks[k][:, half:].astype(BF16), back[:, 2 * width :])
        parts = first[:, 0:1] + first[:, 32:33] + second[:, 64:65] + second[:, 96:97]
        gate = jnp.sum(eye * parts, axis=0, keepdims=True)
        gate_out_ref[k : k + 1, :] = (gate / gate_ref[k : k + 1, :].astype(F32)).astype(BF16)


def call(kernel, outs, args, limit=60, **kw):
    return pl.pallas_call(
        kernel,
        out_shape=outs,
        compiler_params=pltpu.CompilerParams(vmem_limit_bytes=limit << 20),
        **kw,
    )(*args)


LONG = pl.CostEstimate(flops=1 << 40, bytes_accessed=1 << 30, transcendentals=0)


def ranked(values):
    return pl.pallas_call(
        lambda source, result: None,
        out_shape=jax.ShapeDtypeStruct(values.shape, values.dtype),
        in_specs=[pl.BlockSpec(memory_space=pl.ANY)],
        out_specs=pl.BlockSpec(memory_space=pl.ANY),
        input_output_aliases={0: 0},
        compiler_params=pltpu.CompilerParams(vmem_limit_bytes=1 << 20),
        cost_estimate=LONG,
    )(values)


def on_device(moe_input, lm_grad, frame_grad, span_token, expert_ids, gate_weights, w_gate_up, w_down):
    tokens, width = moe_input.shape
    per_span = frame_grad.shape[0] // span_token.shape[0]
    experts = lax.axis_size("expert")
    cap = 2 * tokens * expert_ids.shape[1] // experts
    rows = experts * cap
    half = rows // 2
    ff = w_down.shape[2]
    sds = jax.ShapeDtypeStruct
    any_space = pl.BlockSpec(memory_space=pl.ANY)
    vmem = pl.BlockSpec(memory_space=pltpu.VMEM)
    smem = pl.BlockSpec(memory_space=pltpu.SMEM)

    def exchange(values):
        return lax.all_to_all(
            values.reshape(experts, cap // 2, -1), "expert", split_axis=0, concat_axis=0, tiled=True
        ).reshape(half, -1)

    seq = lax.axis_index("seq")
    place = jnp.stack([seq, lax.axis_index("dp")]).astype(jnp.int32)
    frames = lax.all_gather(frame_grad, "seq", axis=0, tiled=True)

    gates = gate_weights.T
    send_input, target = call(
        functools.partial(route_kernel, experts, cap),
        (sds((half, 2 * width), BF16), sds((2, tokens), jnp.int32)),
        (expert_ids.T, moe_input),
        in_specs=[vmem, any_space],
        out_specs=[any_space, vmem],
        scratch_shapes=[
            pltpu.VMEM((tokens, width), BF16),
            pltpu.VMEM((half, 2 * width), BF16),
            pltpu.SemaphoreType.DMA((5,)),
        ],
    )
    got_input = ranked(exchange(send_input))

    w_gate_up, w_down, target = lax.optimization_barrier((w_gate_up, w_down, target))
    weights = jnp.concatenate([w_gate_up.reshape(-1, 2 * ff), w_down[0]], axis=1)
    weights = lax.all_gather(weights, ("seq", "dp"), axis=0, tiled=True)

    span_token, _ = lax.optimization_barrier((span_token, target))
    names = lax.all_gather(span_token, "seq", axis=0, tiled=True)
    names = jnp.repeat(names, per_span)[None, :]
    send_grad = call(
        upstream_kernel,
        sds((half, 2 * width), BF16),
        ((seq * tokens).reshape(1), names, frames, lm_grad, target, gates),
        in_specs=[smem] + [vmem] * 5,
        cost_estimate=LONG,
    )
    got_grad = exchange(send_grad)

    hidden, gate_term, up_term, columns = call(
        functools.partial(forward_kernel, ff),
        (
            sds((rows, ff), BF16), sds((rows, ff), F32), sds((rows, ff), F32),
            sds((rows, width), BF16),
        ),
        (place, got_input, weights),
        limit=60,
        in_specs=[smem, vmem, vmem],
    )
    input_grad, pre_grad = call(
        functools.partial(backward_kernel, ff),
        (sds((half, 2 * width + 128), BF16), sds((rows, 2 * ff), BF16)),
        (got_grad, weights, hidden, gate_term, up_term),
        in_specs=[any_space] * 5,
        out_specs=[any_space] * 2,
        scratch_shapes=[
            pltpu.VMEM((rows, width), BF16),
            pltpu.VMEM((width, ff), BF16),
            pltpu.VMEM((width, 2 * ff), BF16),
            pltpu.VMEM((rows, ff), BF16),
            pltpu.VMEM((rows, ff), F32),
            pltpu.VMEM((rows, ff), F32),
            pltpu.VMEM((half, 2 * width + 128), BF16),
            pltpu.VMEM((rows, 2 * ff), BF16),
            pltpu.SemaphoreType.DMA((29,)),
        ],
    )
    back = exchange(input_grad)

    partial = mm(columns, pre_grad, TN).astype(BF16)
    other = lax.ppermute(partial[: width // 2], "dp", [(0, 1), (1, 0)])
    pair = (partial[width // 2 :].astype(F32) + other.astype(F32)).astype(BF16)
    grad = lax.psum_scatter(pair, "seq", scatter_dimension=0, tiled=True).astype(F32)
    grad_gate_up = grad.reshape(1, -1, 2, ff)

    grad_input, grad_gates = call(
        combine_kernel,
        (sds((tokens, width), BF16), sds((2, tokens), BF16)),
        (back, target.T, gates),
        limit=20,
        in_specs=[any_space, vmem, vmem],
        out_specs=[vmem, vmem],
        scratch_shapes=[
            pltpu.VMEM((half, 2 * width + 128), BF16),
            pltpu.SemaphoreType.DMA((2,)),
        ],
        cost_estimate=LONG,
    )
    return grad_input, grad_gates.T, grad_gate_up


def solution(mesh):
    every = ("expert", "seq", "dp")
    return jax.shard_map(
        on_device,
        mesh=mesh,
        in_specs=(
            P(every, None),
            P(every, None),
            P(every, None),
            P(every),
            P(every, None),
            P(every, None),
            P("expert", ("seq", "dp"), None, None),
            P("expert", ("seq", "dp"), None),
        ),
        out_specs=(P(every, None), P(every, None), P("expert", ("seq", "dp"), None, None)),
        check_vma=False,
    )
```

```python
import functools

import jax
import jax.numpy as jnp
from jax import lax
from jax.experimental import pallas as pl
from jax.experimental.pallas import tpu as pltpu
from jax.sharding import PartitionSpec as P

F32 = jnp.float32
BF16 = jnp.bfloat16
NT = (((1,), (1,)), ((), ()))
NN = (((1,), (0,)), ((), ()))
TN = (((0,), (0,)), ((), ()))


def mm(a, b, dims=NN):
    return lax.dot_general(a, b, dims, preferred_element_type=F32)


def one_hot(target, rows):
    tokens = target.shape[1]
    return lax.broadcasted_iota(jnp.int32, (rows, tokens), 0) == target


def route_kernel(experts, cap, ids_ref, x_any, send_any, target_ref, x, send, sems):
    load = pltpu.make_async_copy(x_any, x, sems.at[0])
    load.start()
    tokens, width = x.shape
    ids = ids_ref[...]
    members = [
        (lax.broadcasted_iota(jnp.int32, (experts, tokens), 0) == ids[k : k + 1]).astype(F32)
        for k in range(2)
    ]
    earlier = (
        lax.broadcasted_iota(jnp.int32, (tokens, tokens), 0)
        < lax.broadcasted_iota(jnp.int32, (tokens, tokens), 1)
    ).astype(F32)
    count = mm((members[0] + members[1]).astype(BF16), earlier.astype(BF16))
    half = experts * cap // 2
    sub = cap // 2
    targets = []
    for k in range(2):
        position = jnp.sum(members[k] * count, axis=0, keepdims=True).astype(jnp.int32)
        low = jnp.where(position < sub, position, position + (half - sub))
        targets.append(ids[k : k + 1] * sub + low)
        target_ref[k : k + 1, :] = targets[k]
    load.wait()
    block = half // 2
    stores = []
    for j in range(4):
        select = sum(one_hot(t - j * block, block).astype(F32) for t in targets)
        to = (slice(j % 2 * block, (j % 2 + 1) * block), slice(j // 2 * width, (j // 2 + 1) * width))
        send[to] = mm(select.astype(BF16), x[...]).astype(BF16)
        stores.append(pltpu.make_async_copy(send.at[to], send_any.at[to], sems.at[1 + j]))
        stores[j].start()
    for store in stores:
        store.wait()


def upstream_kernel(own_ref, names_ref, frames_ref, lm_ref, target_ref, gate_ref, send_ref):
    tokens = lm_ref.shape[0]
    frames = frames_ref.shape[0]
    own = lax.broadcasted_iota(jnp.int32, (tokens, frames), 0) + own_ref[0]
    named = (own == names_ref[...]).astype(F32)
    cond = mm(named.astype(BF16), frames_ref[...])
    upstream = (lm_ref[...].astype(F32) + cond).astype(BF16)
    half, width = send_ref.shape[0], lm_ref.shape[1]
    hot = [one_hot(target_ref[k : k + 1, :], 2 * half).astype(F32) for k in range(2)]
    gates = gate_ref[...].astype(F32)
    gate = jnp.sum(hot[0] * gates[0:1] + hot[1] * gates[1:2], axis=1, keepdims=True)
    scaled = (mm((hot[0] + hot[1]).astype(BF16), upstream) * gate).astype(BF16)
    send_ref[:, :width] = scaled[:half]
    send_ref[:, width:] = scaled[half:]


def forward_kernel(
    ff, place_ref, x_ref, w_ref, hidden_ref, gate_term_ref, up_term_ref, mine_ref, other_ref
):
    half, width = x_ref.shape[0], x_ref.shape[1] // 2
    core = place_ref[1]
    for i in range(2):
        at = slice(i * half, (i + 1) * half)
        for j in range(width // 256):
            own = pl.ds(pl.multiple_of(i * width + (2 * j + core) * 128, 128), 128)
            away = pl.ds(pl.multiple_of(i * width + (2 * j + 1 - core) * 128, 128), 128)
            mine_ref[at, j * 128 : (j + 1) * 128] = x_ref[:, own]
            other_ref[at, j * 128 : (j + 1) * 128] = x_ref[:, away]
        pre = mm(x_ref[:, i * width : (i + 1) * width], w_ref[:, : 2 * ff])
        gate_pre = pre[:, :ff]
        up_pre = pre[:, ff:]
        sig = jax.nn.sigmoid(gate_pre)
        activated = gate_pre * sig
        slope = sig * (1.0 + gate_pre * (1.0 - sig))
        hidden_ref[at, :] = (activated * up_pre).astype(BF16)
        gate_term_ref[at, :] = up_pre * slope
        up_term_ref[at, :] = activated


def backward_kernel(
    ff, y_any, w_any, hidden_any, gate_any, up_any, out_any, pre_any,
    y, wd, wg, hidden, gate_term, up_term, out, pre, sems,
):
    half, width = y_any.shape[0], y_any.shape[1] // 2
    chunk = width // 4
    copies = []

    def fetch(source, target):
        copies.append(pltpu.make_async_copy(source, target, sems.at[len(copies)]))
        copies[-1].start()

    for c in range(4):
        part = slice(c * chunk, (c + 1) * chunk)
        fetch(w_any.at[part, 2 * ff :], wd.at[part, :])
        for i in range(2):
            begin = i * width + c * chunk
            fetch(y_any.at[:, begin : begin + chunk], y.at[i * half : (i + 1) * half, part])
    hidden_grad = None
    for c in range(4):
        part = slice(c * chunk, (c + 1) * chunk)
        for n in range(3):
            copies[3 * c + n].wait()
        if c == 0:
            fetch(gate_any, gate_term)
            fetch(up_any, up_term)
            fetch(hidden_any, hidden)
        if c == 1:
            for j in range(4):
                to = slice(j * chunk, (j + 1) * chunk)
                fetch(w_any.at[to, : 2 * ff], wg.at[to, :])
        term = mm(y[:, part], wd[part, :])
        hidden_grad = term if hidden_grad is None else hidden_grad + term
    for n in range(12, 19):
        copies[n].wait()
    extra = jnp.zeros((half, 128), F32)
    lane = lax.broadcasted_iota(jnp.int32, (half, 128), 1)
    for i in range(2):
        at = slice(i * half, (i + 1) * half)
        grad = hidden_grad[at]
        pre[at, :ff] = (grad * gate_term[at, :]).astype(BF16)
        pre[at, ff:] = (grad * up_term[at, :]).astype(BF16)
        total = jnp.sum(hidden[at, :].astype(F32) * grad, axis=1, keepdims=True)
        high = total.astype(BF16).astype(F32)
        extra = jnp.where(lane // 64 == i, jnp.where(lane % 64 < 32, high, total - high), extra)
    out[:, 2 * width :] = extra.astype(BF16)
    fetch(out.at[:, 2 * width :], out_any.at[:, 2 * width :])
    for j in range(4):
        grads = mm(pre[...], wg[j * chunk : (j + 1) * chunk, :], NT).astype(BF16)
        for i in range(2):
            to = slice(i * width + j * chunk, i * width + (j + 1) * chunk)
            out[:, to] = grads[i * half : (i + 1) * half]
            fetch(out.at[:, to], out_any.at[:, to])
    fetch(pre, pre_any)
    for copy in copies[19:]:
        copy.wait()

def combine_kernel(back_any, column_ref, gate_ref, out_ref, gate_out_ref, back, sems):
    half = back.shape[0]
    tokens, width = out_ref.shape
    loads = []
    for i, part in enumerate((slice(0, width), slice(width, 2 * width + 128))):
        loads.append(pltpu.make_async_copy(back_any.at[:, part], back.at[:, part], sems.at[i]))
        loads[i].start()
    place = lax.broadcasted_iota(jnp.int32, (tokens, 2 * half), 1)
    picks = [(place == column_ref[:, k : k + 1]).astype(F32) for k in range(2)]
    pick = (picks[0] + picks[1]).astype(BF16)
    loads[0].wait()
    total = mm(pick[:, :half], back[:, :width])
    loads[1].wait()
    total += mm(pick[:, half:], back[:, width : 2 * width])
    out_ref[...] = total.astype(BF16)
    eye = (
        lax.broadcasted_iota(jnp.int32, (tokens, tokens), 0)
        == lax.broadcasted_iota(jnp.int32, (tokens, tokens), 1)
    ).astype(F32)
    for k in range(2):
        first = mm(picks[k][:, :half].astype(BF16), back[:, 2 * width :])
        second = mm(picks[k][:, half:].astype(BF16), back[:, 2 * width :])
        parts = first[:, 0:1] + first[:, 32:33] + second[:, 64:65] + second[:, 96:97]
        gate = jnp.sum(eye * parts, axis=0, keepdims=True)
        gate_out_ref[k : k + 1, :] = (gate / gate_ref[k : k + 1, :].astype(F32)).astype(BF16)


def call(kernel, outs, args, limit=60, **kw):
    return pl.pallas_call(
        kernel,
        out_shape=outs,
        compiler_params=pltpu.CompilerParams(vmem_limit_bytes=limit << 20),
        **kw,
    )(*args)


LONG = pl.CostEstimate(flops=1 << 40, bytes_accessed=1 << 30, transcendentals=0)


def ranked(values):
    return pl.pallas_call(
        lambda source, result: None,
        out_shape=jax.ShapeDtypeStruct(values.shape, values.dtype),
        in_specs=[pl.BlockSpec(memory_space=pl.ANY)],
        out_specs=pl.BlockSpec(memory_space=pl.ANY),
        input_output_aliases={0: 0},
        compiler_params=pltpu.CompilerParams(vmem_limit_bytes=1 << 20),
        cost_estimate=LONG,
    )(values)


def on_device(moe_input, lm_grad, frame_grad, span_token, expert_ids, gate_weights, w_gate_up, w_down):
    tokens, width = moe_input.shape
    per_span = frame_grad.shape[0] // span_token.shape[0]
    experts = lax.axis_size("expert")
    cap = 2 * tokens * expert_ids.shape[1] // experts
    rows = experts * cap
    half = rows // 2
    ff = w_down.shape[2]
    sds = jax.ShapeDtypeStruct
    any_space = pl.BlockSpec(memory_space=pl.ANY)
    vmem = pl.BlockSpec(memory_space=pltpu.VMEM)
    smem = pl.BlockSpec(memory_space=pltpu.SMEM)

    def exchange(values):
        return lax.all_to_all(
            values.reshape(experts, cap // 2, -1), "expert", split_axis=0, concat_axis=0, tiled=True
        ).reshape(half, -1)

    seq = lax.axis_index("seq")
    place = jnp.stack([seq, lax.axis_index("dp")]).astype(jnp.int32)
    frames = lax.all_gather(frame_grad, "seq", axis=0, tiled=True)

    gates = gate_weights.T
    send_input, target = call(
        functools.partial(route_kernel, experts, cap),
        (sds((half, 2 * width), BF16), sds((2, tokens), jnp.int32)),
        (expert_ids.T, moe_input),
        in_specs=[vmem, any_space],
        out_specs=[any_space, vmem],
        scratch_shapes=[
            pltpu.VMEM((tokens, width), BF16),
            pltpu.VMEM((half, 2 * width), BF16),
            pltpu.SemaphoreType.DMA((5,)),
        ],
    )
    got_input = ranked(exchange(send_input))

    w_gate_up, w_down, target = lax.optimization_barrier((w_gate_up, w_down, target))
    weights = jnp.concatenate([w_gate_up.reshape(-1, 2 * ff), w_down[0]], axis=1)
    weights = lax.all_gather(weights, ("seq", "dp"), axis=0, tiled=True)

    span_token, _ = lax.optimization_barrier((span_token, target))
    names = lax.all_gather(span_token, "seq", axis=0, tiled=True)
    names = jnp.repeat(names, per_span)[None, :]
    send_grad = call(
        upstream_kernel,
        sds((half, 2 * width), BF16),
        ((seq * tokens).reshape(1), names, frames, lm_grad, target, gates),
        in_specs=[smem] + [vmem] * 5,
        cost_estimate=LONG,
    )
    got_grad = exchange(send_grad)

    hidden, gate_term, up_term, x_mine, x_other = call(
        functools.partial(forward_kernel, ff),
        (
            sds((rows, ff), BF16), sds((rows, ff), F32), sds((rows, ff), F32),
            sds((rows, width // 2), BF16), sds((rows, width // 2), BF16),
        ),
        (place, got_input, weights),
        limit=60,
        in_specs=[smem, vmem, vmem],
    )
    swap = [(0, 1), (1, 0)]
    x_other = lax.ppermute(x_other, "dp", swap)
    hidden, x_other = lax.optimization_barrier((hidden, x_other))
    input_grad, pre_grad = call(
        functools.partial(backward_kernel, ff),
        (sds((half, 2 * width + 128), BF16), sds((rows, 2 * ff), BF16)),
        (got_grad, weights, hidden, gate_term, up_term),
        in_specs=[any_space] * 5,
        out_specs=[any_space] * 2,
        scratch_shapes=[
            pltpu.VMEM((rows, width), BF16),
            pltpu.VMEM((width, ff), BF16),
            pltpu.VMEM((width, 2 * ff), BF16),
            pltpu.VMEM((rows, ff), BF16),
            pltpu.VMEM((rows, ff), F32),
            pltpu.VMEM((rows, ff), F32),
            pltpu.VMEM((half, 2 * width + 128), BF16),
            pltpu.VMEM((rows, 2 * ff), BF16),
            pltpu.SemaphoreType.DMA((29,)),
        ],
    )
    back = exchange(input_grad)

    pre_other = lax.ppermute(pre_grad, "dp", swap)
    pair = (mm(x_mine, pre_grad, TN) + mm(x_other, pre_other, TN)).astype(BF16)
    grad = lax.psum_scatter(pair, "seq", scatter_dimension=0, tiled=True).astype(F32)
    grad_gate_up = grad.reshape(1, -1, 2, ff)

    grad_input, grad_gates = call(
        combine_kernel,
        (sds((tokens, width), BF16), sds((2, tokens), BF16)),
        (back, target.T, gates),
        limit=20,
        in_specs=[any_space, vmem, vmem],
        out_specs=[vmem, vmem],
        scratch_shapes=[
            pltpu.VMEM((half, 2 * width + 128), BF16),
            pltpu.SemaphoreType.DMA((2,)),
        ],
        cost_estimate=LONG,
    )
    return grad_input, grad_gates.T, grad_gate_up


def solution(mesh):
    every = ("expert", "seq", "dp")
    return jax.shard_map(
        on_device,
        mesh=mesh,
        in_specs=(
            P(every, None),
            P(every, None),
            P(every, None),
            P(every),
            P(every, None),
            P(every, None),
            P("expert", ("seq", "dp"), None, None),
            P("expert", ("seq", "dp"), None),
        ),
        out_specs=(P(every, None), P(every, None), P("expert", ("seq", "dp"), None, None)),
        check_vma=False,
    )
```

```python
import functools

import jax
import jax.numpy as jnp
from jax import lax
from jax.experimental import pallas as pl
from jax.experimental.pallas import tpu as pltpu
from jax.sharding import PartitionSpec as P

F32 = jnp.float32
BF16 = jnp.bfloat16
NT = (((1,), (1,)), ((), ()))
NN = (((1,), (0,)), ((), ()))
TN = (((0,), (0,)), ((), ()))


def mm(a, b, dims=NN):
    return lax.dot_general(a, b, dims, preferred_element_type=F32)


def one_hot(target, rows):
    tokens = target.shape[1]
    return lax.broadcasted_iota(jnp.int32, (rows, tokens), 0) == target


def route_kernel(experts, cap, ids_any, x_any, send_any, target_any, ids_ref, x, send, target, sems):
    names = pltpu.make_async_copy(ids_any, ids_ref, sems.at[0])
    load = pltpu.make_async_copy(x_any, x, sems.at[1])
    names.start()
    load.start()
    tokens, width = x.shape
    earlier = (
        lax.broadcasted_iota(jnp.int32, (tokens, tokens), 0)
        < lax.broadcasted_iota(jnp.int32, (tokens, tokens), 1)
    ).astype(F32)
    names.wait()
    ids = ids_ref[...]
    members = [
        (lax.broadcasted_iota(jnp.int32, (experts, tokens), 0) == ids[k : k + 1]).astype(F32)
        for k in range(2)
    ]
    count = mm((members[0] + members[1]).astype(BF16), earlier.astype(BF16))
    half = experts * cap // 2
    sub = cap // 2
    targets = []
    for k in range(2):
        position = jnp.sum(members[k] * count, axis=0, keepdims=True).astype(jnp.int32)
        low = jnp.where(position < sub, position, position + (half - sub))
        targets.append(ids[k : k + 1] * sub + low)
        target[k : k + 1, :] = targets[k]
    stores = [pltpu.make_async_copy(target, target_any, sems.at[2])]
    stores[0].start()
    load.wait()
    block = half // 2
    for j in range(4):
        select = sum(one_hot(t - j * block, block).astype(F32) for t in targets)
        to = (slice(j % 2 * block, (j % 2 + 1) * block), slice(j // 2 * width, (j // 2 + 1) * width))
        send[to] = mm(select.astype(BF16), x[...]).astype(BF16)
        stores.append(pltpu.make_async_copy(send.at[to], send_any.at[to], sems.at[3 + j]))
        stores[-1].start()
    for store in stores:
        store.wait()


def upstream_kernel(own_ref, names_ref, frames_ref, lm_ref, target_ref, gate_ref, send_ref):
    tokens = lm_ref.shape[0]
    frames = frames_ref.shape[0]
    own = lax.broadcasted_iota(jnp.int32, (tokens, frames), 0) + own_ref[0]
    named = (own == names_ref[...]).astype(F32)
    cond = mm(named.astype(BF16), frames_ref[...])
    upstream = (lm_ref[...].astype(F32) + cond).astype(BF16)
    half, width = send_ref.shape[0], lm_ref.shape[1]
    hot = [one_hot(target_ref[k : k + 1, :], 2 * half).astype(F32) for k in range(2)]
    gates = gate_ref[...].astype(F32)
    gate = jnp.sum(hot[0] * gates[0:1] + hot[1] * gates[1:2], axis=1, keepdims=True)
    scaled = (mm((hot[0] + hot[1]).astype(BF16), upstream) * gate).astype(BF16)
    send_ref[:, :width] = scaled[:half]
    send_ref[:, width:] = scaled[half:]


def forward_kernel(
    ff, place_ref, x_ref, w_ref, hidden_ref, gate_term_ref, up_term_ref, mine_ref, other_ref
):
    half, width = x_ref.shape[0], x_ref.shape[1] // 2
    core = place_ref[1]
    for i in range(2):
        at = slice(i * half, (i + 1) * half)
        for j in range(width // 256):
            own = pl.ds(pl.multiple_of(i * width + (2 * j + core) * 128, 128), 128)
            away = pl.ds(pl.multiple_of(i * width + (2 * j + 1 - core) * 128, 128), 128)
            mine_ref[at, j * 128 : (j + 1) * 128] = x_ref[:, own]
            other_ref[at, j * 128 : (j + 1) * 128] = x_ref[:, away]
        pre = mm(x_ref[:, i * width : (i + 1) * width], w_ref[:, : 2 * ff])
        gate_pre = pre[:, :ff]
        up_pre = pre[:, ff:]
        sig = jax.nn.sigmoid(gate_pre)
        activated = gate_pre * sig
        slope = sig * (1.0 + gate_pre * (1.0 - sig))
        hidden_ref[at, :] = (activated * up_pre).astype(BF16)
        gate_term_ref[at, :] = up_pre * slope
        up_term_ref[at, :] = activated


def backward_kernel(
    ff, y_any, w_any, hidden_any, gate_any, up_any, out_any, pre_any,
    y, wd, wg, hidden, gate_term, up_term, out, pre, sems,
):
    half, width = y_any.shape[0], y_any.shape[1] // 2
    chunk = width // 4
    copies = []

    def fetch(source, target):
        copies.append(pltpu.make_async_copy(source, target, sems.at[len(copies)]))
        copies[-1].start()

    for c in range(4):
        part = slice(c * chunk, (c + 1) * chunk)
        fetch(w_any.at[part, 2 * ff :], wd.at[part, :])
        for i in range(2):
            begin = i * width + c * chunk
            fetch(y_any.at[:, begin : begin + chunk], y.at[i * half : (i + 1) * half, part])
    hidden_grad = None
    for c in range(4):
        part = slice(c * chunk, (c + 1) * chunk)
        for n in range(3):
            copies[3 * c + n].wait()
        if c == 0:
            fetch(gate_any, gate_term)
            fetch(up_any, up_term)
            fetch(hidden_any, hidden)
        if c == 1:
            for j in range(4):
                to = slice(j * chunk, (j + 1) * chunk)
                fetch(w_any.at[to, : 2 * ff], wg.at[to, :])
        term = mm(y[:, part], wd[part, :])
        hidden_grad = term if hidden_grad is None else hidden_grad + term
    for n in range(12, 19):
        copies[n].wait()
    extra = jnp.zeros((half, 128), F32)
    lane = lax.broadcasted_iota(jnp.int32, (half, 128), 1)
    for i in range(2):
        at = slice(i * half, (i + 1) * half)
        grad = hidden_grad[at]
        pre[at, :ff] = (grad * gate_term[at, :]).astype(BF16)
        pre[at, ff:] = (grad * up_term[at, :]).astype(BF16)
        total = jnp.sum(hidden[at, :].astype(F32) * grad, axis=1, keepdims=True)
        high = total.astype(BF16).astype(F32)
        extra = jnp.where(lane // 64 == i, jnp.where(lane % 64 < 32, high, total - high), extra)
    out[:, 2 * width :] = extra.astype(BF16)
    fetch(pre, pre_any)
    fetch(out.at[:, 2 * width :], out_any.at[:, 2 * width :])
    for j in range(4):
        grads = mm(pre[...], wg[j * chunk : (j + 1) * chunk, :], NT).astype(BF16)
        for i in range(2):
            to = slice(i * width + j * chunk, i * width + (j + 1) * chunk)
            out[:, to] = grads[i * half : (i + 1) * half]
            fetch(out.at[:, to], out_any.at[:, to])
    for copy in copies[19:]:
        copy.wait()

def combine_kernel(back_any, column_ref, gate_ref, out_ref, gate_out_ref, back, sems):
    half = back.shape[0]
    tokens, width = out_ref.shape
    loads = []
    for i, part in enumerate((slice(0, width), slice(width, 2 * width + 128))):
        loads.append(pltpu.make_async_copy(back_any.at[:, part], back.at[:, part], sems.at[i]))
        loads[i].start()
    place = lax.broadcasted_iota(jnp.int32, (tokens, 2 * half), 1)
    picks = [(place == column_ref[:, k : k + 1]).astype(F32) for k in range(2)]
    pick = (picks[0] + picks[1]).astype(BF16)
    loads[0].wait()
    total = mm(pick[:, :half], back[:, :width])
    loads[1].wait()
    total += mm(pick[:, half:], back[:, width : 2 * width])
    out_ref[...] = total.astype(BF16)
    eye = (
        lax.broadcasted_iota(jnp.int32, (tokens, tokens), 0)
        == lax.broadcasted_iota(jnp.int32, (tokens, tokens), 1)
    ).astype(F32)
    for k in range(2):
        first = mm(picks[k][:, :half].astype(BF16), back[:, 2 * width :])
        second = mm(picks[k][:, half:].astype(BF16), back[:, 2 * width :])
        parts = first[:, 0:1] + first[:, 32:33] + second[:, 64:65] + second[:, 96:97]
        gate = jnp.sum(eye * parts, axis=0, keepdims=True)
        gate_out_ref[k : k + 1, :] = (gate / gate_ref[k : k + 1, :].astype(F32)).astype(BF16)


def call(kernel, outs, args, limit=60, **kw):
    return pl.pallas_call(
        kernel,
        out_shape=outs,
        compiler_params=pltpu.CompilerParams(vmem_limit_bytes=limit << 20),
        **kw,
    )(*args)


LONG = pl.CostEstimate(flops=1 << 40, bytes_accessed=1 << 30, transcendentals=0)


def ranked(values):
    return pl.pallas_call(
        lambda source, result: None,
        out_shape=jax.ShapeDtypeStruct(values.shape, values.dtype),
        in_specs=[pl.BlockSpec(memory_space=pl.ANY)],
        out_specs=pl.BlockSpec(memory_space=pl.ANY),
        input_output_aliases={0: 0},
        compiler_params=pltpu.CompilerParams(vmem_limit_bytes=1 << 20),
        cost_estimate=LONG,
    )(values)


def on_device(moe_input, lm_grad, frame_grad, span_token, expert_ids, gate_weights, w_gate_up, w_down):
    tokens, width = moe_input.shape
    per_span = frame_grad.shape[0] // span_token.shape[0]
    experts = lax.axis_size("expert")
    cap = 2 * tokens * expert_ids.shape[1] // experts
    rows = experts * cap
    half = rows // 2
    ff = w_down.shape[2]
    sds = jax.ShapeDtypeStruct
    any_space = pl.BlockSpec(memory_space=pl.ANY)
    vmem = pl.BlockSpec(memory_space=pltpu.VMEM)
    smem = pl.BlockSpec(memory_space=pltpu.SMEM)

    def exchange(values):
        return lax.all_to_all(
            values.reshape(experts, cap // 2, -1), "expert", split_axis=0, concat_axis=0, tiled=True
        ).reshape(half, -1)

    seq = lax.axis_index("seq")
    place = jnp.stack([seq, lax.axis_index("dp")]).astype(jnp.int32)
    frames = lax.all_gather(frame_grad, "seq", axis=0, tiled=True)

    gates = gate_weights.T
    send_input, target = call(
        functools.partial(route_kernel, experts, cap),
        (sds((half, 2 * width), BF16), sds((2, tokens), jnp.int32)),
        (expert_ids.T, moe_input),
        in_specs=[any_space] * 2,
        out_specs=[any_space] * 2,
        scratch_shapes=[
            pltpu.VMEM((2, tokens), jnp.int32),
            pltpu.VMEM((tokens, width), BF16),
            pltpu.VMEM((half, 2 * width), BF16),
            pltpu.VMEM((2, tokens), jnp.int32),
            pltpu.SemaphoreType.DMA((7,)),
        ],
    )
    got_input = ranked(exchange(send_input))

    w_gate_up, w_down, target = lax.optimization_barrier((w_gate_up, w_down, target))
    weights = jnp.concatenate([w_gate_up.reshape(-1, 2 * ff), w_down[0]], axis=1)
    weights = lax.all_gather(weights, ("seq", "dp"), axis=0, tiled=True)

    span_token, _ = lax.optimization_barrier((span_token, target))
    names = lax.all_gather(span_token, "seq", axis=0, tiled=True)
    names = jnp.repeat(names, per_span)[None, :]
    send_grad = call(
        upstream_kernel,
        sds((half, 2 * width), BF16),
        ((seq * tokens).reshape(1), names, frames, lm_grad, target, gates),
        in_specs=[smem] + [vmem] * 5,
        cost_estimate=LONG,
    )
    got_grad = exchange(send_grad)

    hidden, gate_term, up_term, x_mine, x_other = call(
        functools.partial(forward_kernel, ff),
        (
            sds((rows, ff), BF16), sds((rows, ff), F32), sds((rows, ff), F32),
            sds((rows, width // 2), BF16), sds((rows, width // 2), BF16),
        ),
        (place, got_input, weights),
        limit=60,
        in_specs=[smem, vmem, vmem],
    )
    swap = [(0, 1), (1, 0)]
    x_other = lax.ppermute(x_other, "dp", swap)
    hidden, x_other = lax.optimization_barrier((hidden, x_other))
    input_grad, pre_grad = call(
        functools.partial(backward_kernel, ff),
        (sds((half, 2 * width + 128), BF16), sds((rows, 2 * ff), BF16)),
        (got_grad, weights, hidden, gate_term, up_term),
        in_specs=[any_space] * 5,
        out_specs=[any_space] * 2,
        scratch_shapes=[
            pltpu.VMEM((rows, width), BF16),
            pltpu.VMEM((width, ff), BF16),
            pltpu.VMEM((width, 2 * ff), BF16),
            pltpu.VMEM((rows, ff), BF16),
            pltpu.VMEM((rows, ff), F32),
            pltpu.VMEM((rows, ff), F32),
            pltpu.VMEM((half, 2 * width + 128), BF16),
            pltpu.VMEM((rows, 2 * ff), BF16),
            pltpu.SemaphoreType.DMA((29,)),
        ],
    )
    back = exchange(input_grad)

    pre_other = lax.ppermute(pre_grad, "dp", swap)
    pair = (mm(x_mine, pre_grad, TN) + mm(x_other, pre_other, TN)).astype(BF16)
    grad = lax.psum_scatter(pair, "seq", scatter_dimension=0, tiled=True).astype(F32)
    grad_gate_up = grad.reshape(1, -1, 2, ff)

    grad_input, grad_gates = call(
        combine_kernel,
        (sds((tokens, width), BF16), sds((2, tokens), BF16)),
        (back, target.T, gates),
        limit=20,
        in_specs=[any_space, vmem, vmem],
        out_specs=[vmem, vmem],
        scratch_shapes=[
            pltpu.VMEM((half, 2 * width + 128), BF16),
            pltpu.SemaphoreType.DMA((2,)),
        ],
        cost_estimate=LONG,
    )
    return grad_input, grad_gates.T, grad_gate_up


def solution(mesh):
    every = ("expert", "seq", "dp")
    return jax.shard_map(
        on_device,
        mesh=mesh,
        in_specs=(
            P(every, None),
            P(every, None),
            P(every, None),
            P(every),
            P(every, None),
            P(every, None),
            P("expert", ("seq", "dp"), None, None),
            P("expert", ("seq", "dp"), None),
        ),
        out_specs=(P(every, None), P(every, None), P("expert", ("seq", "dp"), None, None)),
        check_vma=False,
    )
```

```python
import functools

import jax
import jax.numpy as jnp
from jax import lax
from jax.experimental import pallas as pl
from jax.experimental.pallas import tpu as pltpu
from jax.sharding import PartitionSpec as P

F32 = jnp.float32
BF16 = jnp.bfloat16
NX, NZ = 4, 8
ORDER = [[x * NZ + z for z in range(NZ) for x in range(NX)]]
NT = (((1,), (1,)), ((), ()))
NN = (((1,), (0,)), ((), ()))
TN = (((0,), (0,)), ((), ()))


def mm(a, b, dims=NN):
    return lax.dot_general(a, b, dims, preferred_element_type=F32)


def one_hot(target, rows):
    tokens = target.shape[1]
    return lax.broadcasted_iota(jnp.int32, (rows, tokens), 0) == target


def route_kernel(experts, cap, ids_any, x_any, send_any, target_any, ids_ref, x, send, target, sems):
    names = pltpu.make_async_copy(ids_any, ids_ref, sems.at[0])
    load = pltpu.make_async_copy(x_any, x, sems.at[1])
    names.start()
    load.start()
    tokens, width = x.shape
    earlier = (
        lax.broadcasted_iota(jnp.int32, (tokens, tokens), 0)
        < lax.broadcasted_iota(jnp.int32, (tokens, tokens), 1)
    ).astype(F32)
    names.wait()
    ids = ids_ref[...] % NZ * NX + ids_ref[...] // NZ
    members = [
        (lax.broadcasted_iota(jnp.int32, (experts, tokens), 0) == ids[k : k + 1]).astype(F32)
        for k in range(2)
    ]
    count = mm((members[0] + members[1]).astype(BF16), earlier.astype(BF16))
    half = experts * cap // 2
    sub = cap // 2
    targets = []
    for k in range(2):
        position = jnp.sum(members[k] * count, axis=0, keepdims=True).astype(jnp.int32)
        low = jnp.where(position < sub, position, position + (half - sub))
        targets.append(ids[k : k + 1] * sub + low)
        target[k : k + 1, :] = targets[k]
    stores = [pltpu.make_async_copy(target, target_any, sems.at[2])]
    stores[0].start()
    load.wait()
    block = half // 2
    for j in range(4):
        select = sum(one_hot(t - j * block, block).astype(F32) for t in targets)
        to = (slice(j % 2 * block, (j % 2 + 1) * block), slice(j // 2 * width, (j // 2 + 1) * width))
        send[to] = mm(select.astype(BF16), x[...]).astype(BF16)
        stores.append(pltpu.make_async_copy(send.at[to], send_any.at[to], sems.at[3 + j]))
        stores[-1].start()
    for store in stores:
        store.wait()


def upstream_kernel(own_ref, names_ref, frames_ref, lm_ref, target_ref, gate_ref, send_ref):
    tokens = lm_ref.shape[0]
    frames = frames_ref.shape[0]
    own = lax.broadcasted_iota(jnp.int32, (tokens, frames), 0) + own_ref[0]
    named = (own == names_ref[...]).astype(F32)
    cond = mm(named.astype(BF16), frames_ref[...])
    upstream = (lm_ref[...].astype(F32) + cond).astype(BF16)
    half, width = send_ref.shape[0], lm_ref.shape[1]
    hot = [one_hot(target_ref[k : k + 1, :], 2 * half).astype(F32) for k in range(2)]
    gates = gate_ref[...].astype(F32)
    gate = jnp.sum(hot[0] * gates[0:1] + hot[1] * gates[1:2], axis=1, keepdims=True)
    scaled = (mm((hot[0] + hot[1]).astype(BF16), upstream) * gate).astype(BF16)
    send_ref[:, :width] = scaled[:half]
    send_ref[:, width:] = scaled[half:]


def forward_kernel(
    ff, place_ref, x_ref, w_ref, hidden_ref, gate_term_ref, up_term_ref, mine_ref, other_ref
):
    half, width = x_ref.shape[0], x_ref.shape[1] // 2
    core = place_ref[1]
    for i in range(2):
        at = slice(i * half, (i + 1) * half)
        for j in range(width // 256):
            own = pl.ds(pl.multiple_of(i * width + (2 * j + core) * 128, 128), 128)
            away = pl.ds(pl.multiple_of(i * width + (2 * j + 1 - core) * 128, 128), 128)
            mine_ref[at, j * 128 : (j + 1) * 128] = x_ref[:, own]
            other_ref[at, j * 128 : (j + 1) * 128] = x_ref[:, away]
        pre = mm(x_ref[:, i * width : (i + 1) * width], w_ref[:, : 2 * ff])
        gate_pre = pre[:, :ff]
        up_pre = pre[:, ff:]
        sig = jax.nn.sigmoid(gate_pre)
        activated = gate_pre * sig
        slope = sig * (1.0 + gate_pre * (1.0 - sig))
        hidden_ref[at, :] = (activated * up_pre).astype(BF16)
        gate_term_ref[at, :] = up_pre * slope
        up_term_ref[at, :] = activated


def backward_kernel(
    ff, y_any, w_any, hidden_any, gate_any, up_any, out_any, pre_any,
    y, wd, wg, hidden, gate_term, up_term, out, pre, sems,
):
    half, width = y_any.shape[0], y_any.shape[1] // 2
    chunk = width // 4
    copies = []

    def fetch(source, target):
        copies.append(pltpu.make_async_copy(source, target, sems.at[len(copies)]))
        copies[-1].start()

    for c in range(4):
        part = slice(c * chunk, (c + 1) * chunk)
        fetch(w_any.at[part, 2 * ff :], wd.at[part, :])
        for i in range(2):
            begin = i * width + c * chunk
            fetch(y_any.at[:, begin : begin + chunk], y.at[i * half : (i + 1) * half, part])
    hidden_grad = None
    for c in range(4):
        part = slice(c * chunk, (c + 1) * chunk)
        for n in range(3):
            copies[3 * c + n].wait()
        if c == 0:
            fetch(gate_any, gate_term)
            fetch(up_any, up_term)
            fetch(hidden_any, hidden)
        if c == 1:
            for j in range(4):
                to = slice(j * chunk, (j + 1) * chunk)
                fetch(w_any.at[to, : 2 * ff], wg.at[to, :])
        term = mm(y[:, part], wd[part, :])
        hidden_grad = term if hidden_grad is None else hidden_grad + term
    for n in range(12, 19):
        copies[n].wait()
    extra = jnp.zeros((half, 128), F32)
    lane = lax.broadcasted_iota(jnp.int32, (half, 128), 1)
    for i in range(2):
        at = slice(i * half, (i + 1) * half)
        grad = hidden_grad[at]
        pre[at, :ff] = (grad * gate_term[at, :]).astype(BF16)
        pre[at, ff:] = (grad * up_term[at, :]).astype(BF16)
        total = jnp.sum(hidden[at, :].astype(F32) * grad, axis=1, keepdims=True)
        high = total.astype(BF16).astype(F32)
        extra = jnp.where(lane // 64 == i, jnp.where(lane % 64 < 32, high, total - high), extra)
    out[:, 2 * width :] = extra.astype(BF16)
    fetch(pre, pre_any)
    fetch(out.at[:, 2 * width :], out_any.at[:, 2 * width :])
    for j in range(4):
        grads = mm(pre[...], wg[j * chunk : (j + 1) * chunk, :], NT).astype(BF16)
        for i in range(2):
            to = slice(i * width + j * chunk, i * width + (j + 1) * chunk)
            out[:, to] = grads[i * half : (i + 1) * half]
            fetch(out.at[:, to], out_any.at[:, to])
    for copy in copies[19:]:
        copy.wait()

def combine_kernel(back_any, column_ref, gate_ref, out_ref, gate_out_ref, back, sems):
    half = back.shape[0]
    tokens, width = out_ref.shape
    loads = []
    for i, part in enumerate((slice(0, width), slice(width, 2 * width + 128))):
        loads.append(pltpu.make_async_copy(back_any.at[:, part], back.at[:, part], sems.at[i]))
        loads[i].start()
    place = lax.broadcasted_iota(jnp.int32, (tokens, 2 * half), 1)
    picks = [(place == column_ref[:, k : k + 1]).astype(F32) for k in range(2)]
    pick = (picks[0] + picks[1]).astype(BF16)
    loads[0].wait()
    total = mm(pick[:, :half], back[:, :width])
    loads[1].wait()
    total += mm(pick[:, half:], back[:, width : 2 * width])
    out_ref[...] = total.astype(BF16)
    eye = (
        lax.broadcasted_iota(jnp.int32, (tokens, tokens), 0)
        == lax.broadcasted_iota(jnp.int32, (tokens, tokens), 1)
    ).astype(F32)
    for k in range(2):
        first = mm(picks[k][:, :half].astype(BF16), back[:, 2 * width :])
        second = mm(picks[k][:, half:].astype(BF16), back[:, 2 * width :])
        parts = first[:, 0:1] + first[:, 32:33] + second[:, 64:65] + second[:, 96:97]
        gate = jnp.sum(eye * parts, axis=0, keepdims=True)
        gate_out_ref[k : k + 1, :] = (gate / gate_ref[k : k + 1, :].astype(F32)).astype(BF16)


def call(kernel, outs, args, limit=60, **kw):
    return pl.pallas_call(
        kernel,
        out_shape=outs,
        compiler_params=pltpu.CompilerParams(vmem_limit_bytes=limit << 20),
        **kw,
    )(*args)


LONG = pl.CostEstimate(flops=1 << 40, bytes_accessed=1 << 30, transcendentals=0)


def ranked(values):
    return pl.pallas_call(
        lambda source, result: None,
        out_shape=jax.ShapeDtypeStruct(values.shape, values.dtype),
        in_specs=[pl.BlockSpec(memory_space=pl.ANY)],
        out_specs=pl.BlockSpec(memory_space=pl.ANY),
        input_output_aliases={0: 0},
        compiler_params=pltpu.CompilerParams(vmem_limit_bytes=1 << 20),
        cost_estimate=LONG,
    )(values)


def on_device(moe_input, lm_grad, frame_grad, span_token, expert_ids, gate_weights, w_gate_up, w_down):
    tokens, width = moe_input.shape
    per_span = frame_grad.shape[0] // span_token.shape[0]
    experts = lax.axis_size("expert")
    cap = 2 * tokens * expert_ids.shape[1] // experts
    rows = experts * cap
    half = rows // 2
    ff = w_down.shape[2]
    sds = jax.ShapeDtypeStruct
    any_space = pl.BlockSpec(memory_space=pl.ANY)
    vmem = pl.BlockSpec(memory_space=pltpu.VMEM)
    smem = pl.BlockSpec(memory_space=pltpu.SMEM)

    def exchange(values):
        return lax.all_to_all(
            values.reshape(experts, cap // 2, -1), "expert", split_axis=0, concat_axis=0,
            axis_index_groups=ORDER, tiled=True,
        ).reshape(half, -1)

    seq = lax.axis_index("seq")
    place = jnp.stack([seq, lax.axis_index("dp")]).astype(jnp.int32)
    frames = lax.all_gather(frame_grad, "seq", axis=0, tiled=True)

    gates = gate_weights.T
    send_input, target = call(
        functools.partial(route_kernel, experts, cap),
        (sds((half, 2 * width), BF16), sds((2, tokens), jnp.int32)),
        (expert_ids.T, moe_input),
        in_specs=[any_space] * 2,
        out_specs=[any_space] * 2,
        scratch_shapes=[
            pltpu.VMEM((2, tokens), jnp.int32),
            pltpu.VMEM((tokens, width), BF16),
            pltpu.VMEM((half, 2 * width), BF16),
            pltpu.VMEM((2, tokens), jnp.int32),
            pltpu.SemaphoreType.DMA((7,)),
        ],
    )
    got_input = ranked(exchange(send_input))

    w_gate_up, w_down, target = lax.optimization_barrier((w_gate_up, w_down, target))
    weights = jnp.concatenate([w_gate_up.reshape(-1, 2 * ff), w_down[0]], axis=1)
    weights = lax.all_gather(weights, ("seq", "dp"), axis=0, tiled=True)

    span_token, _ = lax.optimization_barrier((span_token, target))
    names = lax.all_gather(span_token, "seq", axis=0, tiled=True)
    names = jnp.repeat(names, per_span)[None, :]
    send_grad = call(
        upstream_kernel,
        sds((half, 2 * width), BF16),
        ((seq * tokens).reshape(1), names, frames, lm_grad, target, gates),
        in_specs=[smem] + [vmem] * 5,
        cost_estimate=LONG,
    )
    got_grad = exchange(send_grad)

    hidden, gate_term, up_term, x_mine, x_other = call(
        functools.partial(forward_kernel, ff),
        (
            sds((rows, ff), BF16), sds((rows, ff), F32), sds((rows, ff), F32),
            sds((rows, width // 2), BF16), sds((rows, width // 2), BF16),
        ),
        (place, got_input, weights),
        limit=60,
        in_specs=[smem, vmem, vmem],
    )
    swap = [(0, 1), (1, 0)]
    x_other = lax.ppermute(x_other, "dp", swap)
    hidden, x_other = lax.optimization_barrier((hidden, x_other))
    input_grad, pre_grad = call(
        functools.partial(backward_kernel, ff),
        (sds((half, 2 * width + 128), BF16), sds((rows, 2 * ff), BF16)),
        (got_grad, weights, hidden, gate_term, up_term),
        in_specs=[any_space] * 5,
        out_specs=[any_space] * 2,
        scratch_shapes=[
            pltpu.VMEM((rows, width), BF16),
            pltpu.VMEM((width, ff), BF16),
            pltpu.VMEM((width, 2 * ff), BF16),
            pltpu.VMEM((rows, ff), BF16),
            pltpu.VMEM((rows, ff), F32),
            pltpu.VMEM((rows, ff), F32),
            pltpu.VMEM((half, 2 * width + 128), BF16),
            pltpu.VMEM((rows, 2 * ff), BF16),
            pltpu.SemaphoreType.DMA((29,)),
        ],
    )
    back = exchange(input_grad)

    pre_other = lax.ppermute(pre_grad, "dp", swap)
    pair = (mm(x_mine, pre_grad, TN) + mm(x_other, pre_other, TN)).astype(BF16)
    grad = lax.psum_scatter(pair, "seq", scatter_dimension=0, tiled=True).astype(F32)
    grad_gate_up = grad.reshape(1, -1, 2, ff)

    grad_input, grad_gates = call(
        combine_kernel,
        (sds((tokens, width), BF16), sds((2, tokens), BF16)),
        (back, target.T, gates),
        limit=20,
        in_specs=[any_space, vmem, vmem],
        out_specs=[vmem, vmem],
        scratch_shapes=[
            pltpu.VMEM((half, 2 * width + 128), BF16),
            pltpu.SemaphoreType.DMA((2,)),
        ],
        cost_estimate=LONG,
    )
    return grad_input, grad_gates.T, grad_gate_up


def solution(mesh):
    every = ("expert", "seq", "dp")
    return jax.shard_map(
        on_device,
        mesh=mesh,
        in_specs=(
            P(every, None),
            P(every, None),
            P(every, None),
            P(every),
            P(every, None),
            P(every, None),
            P("expert", ("seq", "dp"), None, None),
            P("expert", ("seq", "dp"), None),
        ),
        out_specs=(P(every, None), P(every, None), P("expert", ("seq", "dp"), None, None)),
        check_vma=False,
    )
```
